32 devices in a mesh: groups: 2 (over y), cells: 8 (over z, core), narrow: 2 (over x).
Axes of the slice: x: 2, y: 2, z: 4, core: 2. Of those that a mesh axis runs over, the one named last changes fastest.
Arguments:
- queries: bfloat16 [256, 1024], P(('groups', 'cells', 'narrow')), parts along dimension 0, may hold values from -6 to 6
- probes: int32 [256, 8], P(('groups', 'cells', 'narrow')), parts along dimension 0, may hold values from 0 to 15, all different within a row; in each aligned block of 8 rows (0 to 7, 8 to 15, ...) at most 8 rows name the same one
- cell_slot: int32 [16], replicated, may hold values from 0 to 15, each once
- centroids: float32 [16, 1024], P('cells'), may hold values from -4 to 4
- rotations: bfloat16 [16, 1024, 1024], P('cells', None, 'narrow'), may hold values from -0.1875 to 0.1875
- codebooks: bfloat16 [16, 64, 16, 256], P('cells', 'narrow'), may hold values from -6 to 6
Outputs:
- tables: bfloat16 [16, 2, 128, 64, 256], P(('groups', 'cells'), 'narrow'), parts along dimension 0
The draws below stay inside these ranges and needn't reach their ends.
There are 2 independent parts, one for each index of `groups`. The reference program is written for one: setup_inputs(seed, part) draws one part's arguments, and reference() takes and returns one part's arrays. A program takes and returns all parts, laid end to end along the dimension named above; an argument that names none is the same for every part. Nothing has to cross between parts.
Inputs may be any that keep to these rules, and one draw needn't show every extreme that they name: `probes`: each query names 8 different cells. Among the queries of one aligned block of 8 no cell is named more than 8 times, a bound that some block reaches. `cell_slot`: each storage position is held by exactly one cell.
All inputs are finite; a program needn't handle non-finite values.
Results may differ from the reference program's by a relative error of at most 0.0043.
Values may be sent and summed in bfloat16 or wider, within the bound.
A program may use at most 64 MiB of HBM per device.

```python
import math
import jax
import jax.numpy as jnp
import numpy as np
from jax import lax

D = 1024
M = 64
K = 256
S = 16
PROBES = 8
CELL_DEV = 2
Q_DEV = 8
CELLS = 16
QUERIES = 128
MOST = 8
SLOTS = 128
N_CELLS = 8
N_NARROW = 2


def levels(own_key, shape, pieces, low, largest):
    def one(axis_at, shards_of):
        heights = jax.random.uniform(jax.random.fold_in(jax.random.fold_in(own_key, 6), axis_at), (shards_of,), jnp.float32, low / len(pieces), largest / len(pieces))
        return jnp.repeat(jnp.exp(heights), shape[axis_at] // shards_of).reshape((-1,) + (1,) * (len(shape) - axis_at - 1))

    factor_of = one(*pieces[0])
    for cut in pieces[1:]:
        factor_of = factor_of * one(*cut)
    return factor_of


def assign_block(stream_key, own, number, rows, number_of, top, reach, skew):
    order = jax.random.permutation(stream_key, number_of)
    crowded, usual = load_shares(number_of, rows * top, reach, skew, True), load_shares(number_of, rows * top, reach, skew, False)
    places = jnp.arange(number_of)

    def named(sizes, turn):
        used = int((sizes > 0).sum())
        fixed = max(1, used // 4)
        shifted = fixed + (places - fixed + turn * (used - fixed)) % max(1, number_of - fixed)
        return jnp.zeros((number_of,), jnp.int32).at[order[jnp.where(places < fixed, places, shifted)]].set(jnp.asarray(sizes, jnp.int32))

    sizes = jnp.where(number % 4 == 0, named(crowded, number // 4), named(usual, number - number // 4 - 1))
    mixed = jax.random.permutation(jax.random.fold_in(own, 3), number_of)
    giver, sink = mixed[0:number_of // 2 * 2:2], mixed[1:number_of // 2 * 2:2]
    room = jnp.minimum(sizes[giver] - 1, reach - sizes[sink]) // 2
    room = jnp.where((giver == order[0]) | (sink == order[0]) | (sizes[sink] == 0), 0, jnp.maximum(room, 0))
    shifted = jax.random.randint(jax.random.fold_in(own, 4), (number_of // 2,), 0, 1 << 20) % (room + 1)
    sizes = sizes.at[giver].add(-shifted).at[sink].add(shifted)
    labels = jnp.searchsorted(jnp.cumsum(sizes), jnp.arange(rows * top), side="right").astype(jnp.int32)
    listing = labels.reshape(top, rows).T
    listing = listing[jax.random.permutation(jax.random.fold_in(own, 1), rows)]
    turn = jax.random.randint(jax.random.fold_in(own, 2), (rows, 1), 0, top)
    return jnp.take_along_axis(listing, (jnp.arange(top)[None, :] + turn) % top, axis=1)


def load_shares(count, total, bound, lean, full):
    weights = [(1 << 20) // math.isqrt(grade ** lean) + 1 for grade in range(1, count + 1)]
    largest = bound if full else min(bound, max(-(-total // count), total * weights[0] // sum(weights)))
    least = 1 if total - largest >= count - 1 else 0
    given, surplus = [largest] + [least] * (count - 1), total - largest - least * (count - 1)
    while surplus > 0:
        movable = [i for i in range(1, count) if given[i] < largest] or [i for i in range(1, count) if given[i] < bound]
        whole, remaining = sum([weights[i] for i in movable]), surplus
        for i in movable:
            more = min(bound - given[i], max(1, remaining * weights[i] // whole), surplus)
            given[i] = given[i] + more
            surplus = surplus - more
    return np.array(given)


def bell_draw(own_key, shape, width, bound, split=(), kind=jnp.bfloat16):
    drawn = width * jax.random.normal(own_key, shape, jnp.float32)
    if split:
        drawn = drawn * levels(own_key, shape, split, -0.22, 0.18)
    return jnp.clip(drawn, -bound, bound).astype(kind)


def setup_inputs(seed: int = 0, part: int = 0) -> dict:
    arg_keys = jax.random.split(jax.random.key(seed), 7)
    part_splits = jax.random.split(jax.random.fold_in(arg_keys[6], part), 7)
    queries = bell_draw(part_splits[0], (QUERIES, D), 1.0, 6.0, ((0, 16),))
    probes_keys = jax.random.split(jax.random.fold_in(part_splits[1], 1), QUERIES // Q_DEV)
    probes_turns = jax.random.permutation(jax.random.fold_in(part_splits[1], 3), QUERIES // Q_DEV)
    probes = jax.vmap(lambda own, number: assign_block(jax.random.fold_in(part_splits[1], 2), own, number, Q_DEV, CELLS, PROBES, MOST, 2))(probes_keys, probes_turns).reshape((QUERIES, PROBES))
    cell_slot = jax.random.permutation(arg_keys[2], CELLS).astype(jnp.int32)
    centroids = bell_draw(arg_keys[3], (CELLS, D), 0.5, 4.0, ((0, 8),), jnp.float32)
    rotations = bell_draw(arg_keys[4], (CELLS, D, D), D ** -0.5, 0.1875, ((0, 8), (2, 2)))
    codebooks = bell_draw(arg_keys[5], (CELLS, M, S, K), 1.0, 6.0, ((0, 8), (1, 2)))
    return {"queries": queries, "probes": probes, "cell_slot": cell_slot, "centroids": centroids, "rotations": rotations, "codebooks": codebooks}


def subspace_tables(rotated, books):
    parts = rotated.astype(jnp.float32).reshape(rotated.shape[:-1] + (M, S))
    cross = jnp.einsum('ilsmt,lmtk->ilsmk', parts, books.astype(jnp.float32))
    own = jnp.sum(parts * parts, axis=-1)
    word = jnp.sum(jnp.square(books.astype(jnp.float32)), axis=2)
    return (own[..., None] - 2.0 * cross + word[None, :, None, :, :]) / S


def reference(queries, probes, cell_slot, centroids, rotations, codebooks):
    blocks = N_CELLS * N_NARROW
    span = jnp.arange(CELLS, dtype=jnp.int32)

    def route(block_queries, block_probes):
        position = cell_slot[block_probes].reshape(-1)
        hot = (position[:, None] == span[None, :]).astype(jnp.int32)
        rank = jnp.sum((jnp.cumsum(hot, axis=0) - hot) * hot, axis=1)
        slot = position * MOST + rank
        rows = jnp.zeros((CELLS * MOST, D), jnp.bfloat16).at[slot].set(jnp.repeat(block_queries, PROBES, axis=0))
        marks = jnp.zeros((CELLS * MOST,), jnp.float32).at[slot].set(1.0)
        return rows, marks

    rows, marks = jax.vmap(route)(queries.reshape(blocks, Q_DEV, D), probes.reshape(blocks, Q_DEV, PROBES))
    rows = rows.reshape(N_CELLS, N_NARROW, N_CELLS, CELL_DEV, MOST, D).transpose(2, 1, 0, 3, 4, 5)
    marks = marks.reshape(N_CELLS, N_NARROW, N_CELLS, CELL_DEV, MOST).transpose(2, 1, 0, 3, 4)

    def owner_tables(index):
        owner = index // N_NARROW
        narrow = index % N_NARROW
        first = (owner * CELL_DEV).astype(jnp.int32)
        own_rows = rows[owner, narrow]
        own_marks = marks[owner, narrow]
        centre = lax.dynamic_slice_in_dim(centroids, first, CELL_DEV, 0)
        turn = lax.dynamic_slice_in_dim(rotations, first, CELL_DEV, 0)
        books = lax.dynamic_slice_in_dim(codebooks, first, CELL_DEV, 0)
        residual = (own_rows.astype(jnp.float32) - centre[None, :, None, :]).astype(jnp.bfloat16)
        rotated = jnp.einsum('ilsd,lde->ilse', residual.astype(jnp.float32), turn.astype(jnp.float32)).astype(jnp.bfloat16)
        table = subspace_tables(rotated, books) * own_marks[..., None, None]
        return table.astype(jnp.bfloat16).reshape(SLOTS, M, K)

    result = lax.map(owner_tables, jnp.arange(blocks, dtype=jnp.int32))
    return result.reshape(N_CELLS, N_NARROW, SLOTS, M, K)
```

```python
import functools

import jax
import jax.numpy as jnp
from jax import lax
from jax.experimental import pallas as pl
from jax.experimental.pallas import tpu as pltpu
from jax.sharding import PartitionSpec as P

MESH = pl.DeviceIdType.MESH
F32 = jnp.float32
BF16 = jnp.bfloat16
LANES = 128


def most_of(q_dev, probe_count, cells_all):
    return min(q_dev, max(2, 2 * q_dev * probe_count // cells_all))


def exchange_kernel(
    owners, most, slot_of, queries, probes, centroids, rotations, books,
    x_out, books_out, marks_out,
    blocks, turn, x_send, q_send_sem, q_recv_sem, b_sem, r_sem, local_sem,
):
    q_dev, depth = queries.shape
    probe_count = probes.shape[1]
    cell_dev, half_m = books.shape[:2]
    half = rotations.shape[2]
    cells_all = slot_of.shape[0]
    rows = owners * q_dev
    slots = owners * most
    g = lax.axis_index("groups")
    j = lax.axis_index("cells")
    n = lax.axis_index("narrow")
    other = 1 - n

    load = pltpu.make_async_copy(rotations, turn, local_sem.at[0])
    load.start()
    keep = pltpu.make_async_copy(
        books, books_out.at[:, pl.ds(n * half_m, half_m)], local_sem.at[1]
    )
    keep.start()

    peers = [(dj, dn) for dn in (1, 0) for dj in range(owners) if (dj, dn) != (0, 0)]

    def target(dj, dn):
        return (g, lax.rem(j + dj, owners), lax.rem(n + dn, 2))

    barrier = pltpu.get_barrier_semaphore()
    for dj, dn in peers:
        pl.semaphore_signal(barrier, inc=1, device_id=target(dj, dn), device_id_type=MESH)

    blocks[n, j, :, :depth] = queries[...]
    tail = jnp.concatenate(
        [probes[...].astype(F32), jnp.zeros((q_dev, LANES - probe_count), F32)], axis=1
    )
    blocks[n, j, :, depth:] = tail.astype(BF16)
    pl.semaphore_wait(barrier, len(peers))

    sends = []
    for k, (dj, dn) in enumerate(peers):
        copy = pltpu.make_async_remote_copy(
            src_ref=blocks.at[n, j],
            dst_ref=blocks.at[n, j],
            send_sem=q_send_sem.at[k],
            recv_sem=q_recv_sem.at[k],
            device_id=target(dj, dn),
            device_id_type=MESH,
        )
        copy.start()
        sends.append(copy)
    mine = pl.ds(n * half_m, half_m)
    books_copy = pltpu.make_async_remote_copy(
        src_ref=books,
        dst_ref=books_out.at[:, mine],
        send_sem=b_sem.at[0],
        recv_sem=b_sem.at[1],
        device_id=(g, j, other),
        device_id_type=MESH,
    )
    books_copy.start()

    def arrived(dn):
        for k, (dj, kn) in enumerate(peers):
            if kn == dn:
                source = blocks.at[lax.rem(n + 2 - dn, 2), lax.rem(j + owners - dj, owners)]
                pltpu.make_async_remote_copy(
                    src_ref=source,
                    dst_ref=source,
                    send_sem=q_send_sem.at[k],
                    recv_sem=q_recv_sem.at[k],
                    device_id=target(dj, dn),
                    device_id_type=MESH,
                ).wait_recv()

    row = lax.broadcasted_iota(jnp.int32, (rows, rows), 0)
    col = lax.broadcasted_iota(jnp.int32, (rows, rows), 1)
    earlier = ((row < col) & (row // q_dev == col // q_dev)).astype(F32).astype(BF16)
    slot_row = lax.broadcasted_iota(jnp.int32, (slots, rows), 0)
    slot_col = lax.broadcasted_iota(jnp.int32, (slots, rows), 1)
    same = (slot_row // most == slot_col // q_dev).astype(F32)
    place = (slot_row % most).astype(F32)

    def cell_at(position):
        cell = jnp.int32(0)
        for c in range(cells_all):
            cell = cell + jnp.where(slot_of[c] == position, c, 0)
        return cell

    cells = [cell_at(j * cell_dev + l).astype(F32) for l in range(cell_dev)]

    def column(which):
        wide = blocks[which].astype(F32).reshape(rows, depth + LANES)
        named = wide[:, depth:]
        lane = lax.broadcasted_iota(jnp.int32, (rows, LANES), 1) < probe_count
        out = []
        for l in range(cell_dev):
            hit = ((named == cells[l]) & lane).astype(F32).astype(BF16)
            hits = lax.dot_general(
                jnp.ones((8, LANES), BF16), hit, (((1,), (1,)), ((), ())),
                preferred_element_type=F32,
            )
            rank = jnp.dot(hits.astype(BF16), earlier, preferred_element_type=F32)
            pick = (place == rank[:1]).astype(F32) * hits[:1] * same
            residual = (wide[:, :depth] - centroids[l : l + 1]).astype(BF16)
            rotated = jnp.dot(residual, turn[l], preferred_element_type=F32).astype(BF16)
            x = jnp.dot(pick.astype(BF16), rotated, preferred_element_type=F32).astype(BF16)
            out.append((x, pick))
        return out

    here = pl.ds(pl.multiple_of(n * half, LANES), half)
    load.wait()
    arrived(1)
    for l, (x, _) in enumerate(column(other)):
        x_send[l] = x
    x_copy = pltpu.make_async_remote_copy(
        src_ref=x_send,
        dst_ref=x_out.at[:, :, here],
        send_sem=r_sem.at[0],
        recv_sem=r_sem.at[1],
        device_id=(g, j, other),
        device_id_type=MESH,
    )
    x_copy.start()
    arrived(0)
    for l, (x, pick) in enumerate(column(n)):
        x_out[l, :, here] = x
        marks_out[l] = jnp.broadcast_to(
            jnp.sum(pick, axis=1, keepdims=True), marks_out.shape[1:]
        )
    keep.wait()
    for copy in sends:
        copy.wait_send()
    x_copy.wait()
    books_copy.wait()


def table_kernel(x_ref, books_ref, marks_ref, out_ref):
    _, group, width, words = books_ref.shape
    slots, span = x_ref.shape[1:]
    blocks, _, most = out_ref.shape[:3]
    lane = lax.broadcasted_iota(jnp.int32, (group, span), 1)
    row = lax.broadcasted_iota(jnp.int32, (group, span), 0)
    mask = (lane // width == row).astype(F32)
    book = books_ref[0].reshape(group * width, words)
    wide = books_ref[0].astype(F32)
    word = jnp.sum(wide * wide, axis=1)
    x = x_ref[0].astype(F32)
    spread = x[:, None, :] * mask[None]
    own = jnp.sum(spread * spread, axis=2, keepdims=True)
    cross = jnp.dot(
        spread.astype(BF16).reshape(slots * group, span), book, preferred_element_type=F32
    ).reshape(slots, group, words)
    marks = marks_ref[0] * (1.0 / width)
    table = (own - 2.0 * cross + word[None]) * marks[:, None, :]
    out_ref[...] = table.astype(BF16).reshape(blocks, 1, most, group, words)


def two_narrow(queries, probes, cell_slot, centroids, rotations, codebooks):
    q_dev, probe_count = probes.shape
    cells_all = cell_slot.shape[0]
    cell_dev, half_m, width, words = codebooks.shape
    depth = queries.shape[1]
    half = rotations.shape[2]
    owners = lax.axis_size("cells")
    most = most_of(q_dev, probe_count, cells_all)
    slots = owners * most
    peers = 2 * owners - 1
    vmem = pl.BlockSpec(memory_space=pltpu.VMEM)
    anywhere = pl.BlockSpec(memory_space=pl.ANY)
    x, books, marks = pl.pallas_call(
        functools.partial(exchange_kernel, owners, most),
        name="exchange",
        out_shape=(
            jax.ShapeDtypeStruct((cell_dev, slots, depth), BF16),
            jax.ShapeDtypeStruct((cell_dev, 2 * half_m, width, words), BF16),
            jax.ShapeDtypeStruct((cell_dev, slots, words), F32),
        ),
        in_specs=[
            pl.BlockSpec(memory_space=pltpu.SMEM), vmem, vmem, vmem, anywhere, anywhere,
        ],
        out_specs=(vmem, anywhere, vmem),
        scratch_shapes=[
            pltpu.VMEM((2, owners, q_dev, depth + LANES), BF16),
            pltpu.VMEM(rotations.shape, BF16),
            pltpu.VMEM((cell_dev, slots, half), BF16),
            pltpu.SemaphoreType.DMA((peers,)),
            pltpu.SemaphoreType.DMA((peers,)),
            pltpu.SemaphoreType.DMA((2,)),
            pltpu.SemaphoreType.DMA((2,)),
            pltpu.SemaphoreType.DMA((2,)),
        ],
        compiler_params=pltpu.CompilerParams(
            collective_id=0, has_side_effects=True, vmem_limit_bytes=32 << 20
        ),
    )(cell_slot, queries, probes, centroids, rotations, codebooks)

    group = 16
    groups = 2 * half_m // group
    table = pl.pallas_call(
        table_kernel,
        name="tables",
        grid=(cell_dev, groups),
        out_shape=jax.ShapeDtypeStruct(
            (owners, cell_dev, most, 2 * half_m, words), BF16
        ),
        in_specs=[
            pl.BlockSpec((1, slots, group * width), lambda l, m: (l, 0, m)),
            pl.BlockSpec((1, group, width, words), lambda l, m: (l, m, 0, 0)),
            pl.BlockSpec((1, slots, words), lambda l, m: (l, 0, 0)),
        ],
        out_specs=pl.BlockSpec(
            (owners, 1, most, group, words), lambda l, m: (0, l, 0, m, 0)
        ),
        compiler_params=pltpu.CompilerParams(vmem_limit_bytes=32 << 20),
    )(x, books, marks)
    return table.reshape(1, 1, owners * cell_dev * most, 2 * half_m, words)


def subspace_tables(rotated, books):
    width = books.shape[2]
    parts = rotated.reshape(rotated.shape[:-1] + (books.shape[1], width))
    cross = jnp.einsum("...lsmt,lmtk->...lsmk", parts, books, preferred_element_type=F32)
    wide = parts.astype(F32)
    own = jnp.sum(wide * wide, axis=-1)
    word = jnp.sum(jnp.square(books.astype(F32)), axis=2)
    return (own[..., None] - 2.0 * cross + word[:, None, :, :]) / width


def any_narrow(queries, probes, cell_slot, centroids, rotations, codebooks):
    q_dev, probe_count = probes.shape
    cells_all = cell_slot.shape[0]
    cell_dev = centroids.shape[0]
    depth = queries.shape[1]
    most = most_of(q_dev, probe_count, cells_all)
    owners = lax.axis_size("cells")
    span = jnp.arange(cells_all, dtype=jnp.int32)
    owner_hot = (cell_slot[:, None] == span[None, :]).astype(jnp.int32)
    probe_hot = (probes.reshape(-1)[:, None] == span[None, :]).astype(jnp.int32)
    position_hot = jnp.dot(probe_hot, owner_hot)
    rank = jnp.sum((jnp.cumsum(position_hot, axis=0) - position_hot) * position_hot, axis=1)
    position = jnp.dot(position_hot, span)
    slot = position * most + rank
    slot_span = jnp.arange(cells_all * most, dtype=jnp.int32)
    assign = jnp.sum(
        (slot[:, None] == slot_span[None, :])
        .astype(jnp.int32)
        .reshape(q_dev, probe_count, cells_all * most),
        axis=1,
    )
    send = jnp.einsum(
        "qs,qd->sd", assign.astype(BF16), queries, preferred_element_type=F32
    ).astype(BF16)
    valid = jnp.sum(assign, axis=0).astype(BF16)
    rows = lax.all_to_all(
        send.reshape(owners, cell_dev * most, depth), "cells", split_axis=0, concat_axis=0, tiled=True
    ).reshape(owners, cell_dev, most, depth)
    marks = lax.all_to_all(
        valid.reshape(owners, cell_dev * most), "cells", split_axis=0, concat_axis=0, tiled=True
    ).reshape(owners, cell_dev, most)
    residual = (rows.astype(F32) - centroids[None, :, None, :]).astype(BF16)
    rotated = jnp.einsum(
        "nilsd,lde->nilse",
        lax.all_gather(residual[None], "narrow", axis=0, tiled=True),
        rotations,
        preferred_element_type=F32,
    ).astype(BF16)
    gathered = subspace_tables(rotated, codebooks).astype(BF16)
    mine = lax.all_to_all(gathered, "narrow", split_axis=0, concat_axis=4, tiled=True)[0]
    table = mine * marks[..., None, None]
    return table.reshape((1, 1, owners * cell_dev * most) + table.shape[-2:])


def solution(mesh):
    return jax.shard_map(
        two_narrow if mesh.shape["narrow"] == 2 else any_narrow,
        mesh=mesh,
        in_specs=(
            P(("groups", "cells", "narrow"), None),
            P(("groups", "cells", "narrow"), None),
            P(),
            P("cells", None),
            P("cells", None, "narrow"),
            P("cells", "narrow", None, None),
        ),
        out_specs=P(("groups", "cells"), "narrow", None, None, None),
        check_vma=False,
    )
```

```python
import functools

import jax
import jax.numpy as jnp
from jax import lax
from jax.experimental import pallas as pl
from jax.experimental.pallas import tpu as pltpu
from jax.sharding import PartitionSpec as P

MESH = pl.DeviceIdType.MESH
F32 = jnp.float32
BF16 = jnp.bfloat16
LANES = 128


def most_of(q_dev, probe_count, cells_all):
    return min(q_dev, max(2, 2 * q_dev * probe_count // cells_all))


def exchange_kernel(
    owners, most, slot_hbm, queries_hbm, probes_hbm, centroids_hbm, rotations, books,
    x_out, books_out, marks_out,
    blocks, turn, x_send, slot_of, probes, centroids,
    q_send_sem, q_recv_sem, b_send_sem, b_recv_sem, y_send_sem, y_recv_sem, r_sem, local_sem,
):
    q_dev, depth = queries_hbm.shape
    probe_count = probes.shape[1]
    cell_dev, half_m = books.shape[:2]
    half = rotations.shape[2]
    cells_all = slot_of.shape[0]
    rows = owners * q_dev
    slots = owners * most
    pieces = b_send_sem.shape[0]
    step = half_m // pieces
    g = lax.axis_index("groups")
    j = lax.axis_index("cells")
    n = lax.axis_index("narrow")
    other = 1 - n

    peers = [(dj, dn) for dn in (1, 0) for dj in range(owners) if (dj, dn) != (0, 0)]

    def target(dj, dn):
        return (g, lax.rem(j + dj, owners), lax.rem(n + dn, 2))

    across = (1 - g, j, n)
    barrier = pltpu.get_barrier_semaphore()
    for dj, dn in peers:
        pl.semaphore_signal(barrier, inc=1, device_id=target(dj, dn), device_id_type=MESH)
    pl.semaphore_signal(barrier, inc=1, device_id=across, device_id_type=MESH)

    loads = [
        pltpu.make_async_copy(src, dst, local_sem.at[i])
        for i, (src, dst) in enumerate(
            [
                (queries_hbm, blocks.at[n, j, :, pl.ds(0, depth)]),
                (probes_hbm, probes),
                (slot_hbm, slot_of),
                (centroids_hbm, centroids),
                (rotations, turn),
                (books, books_out.at[:, pl.ds(n * half_m, half_m)]),
            ]
        )
    ]
    for load in loads:
        load.start()
    loads[1].wait()
    tail = jnp.concatenate(
        [probes[...].astype(F32), jnp.zeros((q_dev, LANES - probe_count), F32)], axis=1
    )
    blocks[n, j, :, depth:] = tail.astype(BF16)
    loads[0].wait()
    pl.semaphore_wait(barrier, len(peers) + 1)

    sends = []
    for k, (dj, dn) in enumerate(peers):
        copy = pltpu.make_async_remote_copy(
            src_ref=blocks.at[n, j],
            dst_ref=blocks.at[n, j],
            send_sem=q_send_sem.at[k],
            recv_sem=q_recv_sem.at[k],
            device_id=target(dj, dn),
            device_id_type=MESH,
        )
        copy.start()
        sends.append(copy)
    firsts = []
    for p in range(pieces):
        copy = pltpu.make_async_remote_copy(
            src_ref=books.at[g, pl.ds(p * step, step)],
            dst_ref=books_out.at[g, pl.ds(n * half_m + p * step, step)],
            send_sem=b_send_sem.at[p],
            recv_sem=b_recv_sem.at[p],
            device_id=(g, j, other),
            device_id_type=MESH,
        )
        copy.start()
        firsts.append(copy)
    relays = []

    def relay(p):
        firsts[p].wait_recv()
        piece = books_out.at[g, pl.ds(other * half_m + p * step, step)]
        copy = pltpu.make_async_remote_copy(
            src_ref=piece,
            dst_ref=piece,
            send_sem=y_send_sem.at[p],
            recv_sem=y_recv_sem.at[p],
            device_id=across,
            device_id_type=MESH,
        )
        copy.start()
        relays.append(copy)

    def arrived(dn):
        for k, (dj, kn) in enumerate(peers):
            if kn == dn:
                source = blocks.at[lax.rem(n + 2 - dn, 2), lax.rem(j + owners - dj, owners)]
                pltpu.make_async_remote_copy(
                    src_ref=source,
                    dst_ref=source,
                    send_sem=q_send_sem.at[k],
                    recv_sem=q_recv_sem.at[k],
                    device_id=target(dj, dn),
                    device_id_type=MESH,
                ).wait_recv()

    row = lax.broadcasted_iota(jnp.int32, (rows, rows), 0)
    col = lax.broadcasted_iota(jnp.int32, (rows, rows), 1)
    earlier = ((row < col) & (row // q_dev == col // q_dev)).astype(F32).astype(BF16)
    slot_row = lax.broadcasted_iota(jnp.int32, (slots, rows), 0)
    slot_col = lax.broadcasted_iota(jnp.int32, (slots, rows), 1)
    same = (slot_row // most == slot_col // q_dev).astype(F32)
    place = (slot_row % most).astype(F32)

    def cell_at(position):
        cell = jnp.int32(0)
        for c in range(cells_all):
            cell = cell + jnp.where(slot_of[c] == position, c, 0)
        return cell

    loads[2].wait()
    loads[3].wait()
    cells = [cell_at(j * cell_dev + l).astype(F32) for l in range(cell_dev)]

    def column(which):
        wide = blocks[which].astype(F32).reshape(rows, depth + LANES)
        named = wide[:, depth:]
        lane = lax.broadcasted_iota(jnp.int32, (rows, LANES), 1) < probe_count
        out = []
        for l in range(cell_dev):
            hit = ((named == cells[l]) & lane).astype(F32).astype(BF16)
            hits = lax.dot_general(
                jnp.ones((8, LANES), BF16), hit, (((1,), (1,)), ((), ())),
                preferred_element_type=F32,
            )
            rank = jnp.dot(hits.astype(BF16), earlier, preferred_element_type=F32)
            pick = (place == rank[:1]).astype(F32) * hits[:1] * same
            residual = (wide[:, :depth] - centroids[l : l + 1]).astype(BF16)
            rotated = jnp.dot(residual, turn[l], preferred_element_type=F32).astype(BF16)
            x = jnp.dot(pick.astype(BF16), rotated, preferred_element_type=F32).astype(BF16)
            out.append((x, pick))
        return out

    here = pl.ds(pl.multiple_of(n * half, LANES), half)
    for p in range(pieces // 2):
        relay(p)
    loads[4].wait()
    arrived(1)
    for l, (x, _) in enumerate(column(other)):
        x_send[l] = x
    x_copy = pltpu.make_async_remote_copy(
        src_ref=x_send,
        dst_ref=x_out.at[:, :, here],
        send_sem=r_sem.at[0],
        recv_sem=r_sem.at[1],
        device_id=(g, j, other),
        device_id_type=MESH,
    )
    x_copy.start()
    for p in range(pieces // 2, pieces):
        relay(p)
    arrived(0)
    for l, (x, pick) in enumerate(column(n)):
        x_out[l, :, here] = x
        marks_out[l] = jnp.broadcast_to(
            jnp.sum(pick, axis=1, keepdims=True), marks_out.shape[1:]
        )
    loads[5].wait()
    for copy in sends + firsts:
        copy.wait_send()
    x_copy.wait()
    for copy in relays:
        copy.wait()


def split3(value):
    high = value.astype(BF16)
    rest = value - high.astype(F32)
    middle = rest.astype(BF16)
    low = (rest - middle.astype(F32)).astype(BF16)
    return high, middle, low


def table_kernel(x_ref, books_ref, marks_ref, out_ref):
    _, group, width, words = books_ref.shape
    slots, span = x_ref.shape[1:]
    blocks, _, most = out_ref.shape[:3]
    scale = 1.0 / width
    extra = LANES
    third = 3 * group
    lane = lax.broadcasted_iota(jnp.int32, (group, span + extra), 1)
    row = lax.broadcasted_iota(jnp.int32, (group, span + extra), 0)
    mask = (jnp.where(lane < span, lane // width, lane % group) == row).astype(F32)

    wide = books_ref[0].astype(F32)
    word = jnp.sum(wide * wide, axis=1) * scale
    book = jnp.concatenate(
        [
            books_ref[0].reshape(group * width, words),
            *split3(word),
            jnp.ones((third, words), BF16),
            jnp.zeros((extra - 2 * third, words), BF16),
        ],
        axis=0,
    )

    x = x_ref[0].astype(F32)
    square = x * x
    high = square.astype(BF16)
    low = (square - high.astype(F32)).astype(BF16)
    at = lax.broadcasted_iota(jnp.int32, (span, extra), 0) // width
    to = lax.broadcasted_iota(jnp.int32, (span, extra), 1)
    gather = ((to % group == at) & (to >= third) & (to < 2 * third)).astype(F32)
    gather = gather.astype(BF16)
    own = scale * (
        jnp.dot(high, gather, preferred_element_type=F32)
        + jnp.dot(low, gather, preferred_element_type=F32)
    )
    tops = [part.astype(F32) for part in split3(own)]
    spot = lax.broadcasted_iota(jnp.int32, (slots, extra), 1)
    part = jnp.where(spot < third + group, tops[0], jnp.where(spot < third + 2 * group, tops[1], tops[2]))
    part = jnp.where(spot < third, marks_ref[0], part)
    left = jnp.concatenate([x * (-2.0 * scale), part], axis=1)
    spread = (left[:, None, :] * mask[None]).astype(BF16).reshape(slots * group, span + extra)
    table = jnp.dot(spread, book, preferred_element_type=F32)
    out_ref[...] = table.astype(BF16).reshape(blocks, 1, most, group, words)


def two_narrow(queries, probes, cell_slot, centroids, rotations, codebooks):
    q_dev, probe_count = probes.shape
    cells_all = cell_slot.shape[0]
    cell_dev, half_m, width, words = codebooks.shape
    depth = queries.shape[1]
    half = rotations.shape[2]
    owners = lax.axis_size("cells")
    most = most_of(q_dev, probe_count, cells_all)
    slots = owners * most
    peers = 2 * owners - 1
    vmem = pl.BlockSpec(memory_space=pltpu.VMEM)
    pieces = 4
    x, books, marks = pl.pallas_call(
        functools.partial(exchange_kernel, owners, most),
        name="exchange",
        out_shape=(
            jax.ShapeDtypeStruct((cell_dev, slots, depth), BF16),
            jax.ShapeDtypeStruct((cell_dev, 2 * half_m, width, words), BF16),
            jax.ShapeDtypeStruct((cell_dev, slots, LANES), F32),
        ),
        in_specs=[pl.BlockSpec(memory_space=pltpu.HBM)] * 6,
        out_specs=(vmem, pl.BlockSpec(memory_space=pl.ANY), vmem),
        scratch_shapes=[
            pltpu.VMEM((2, owners, q_dev, depth + LANES), BF16),
            pltpu.VMEM(rotations.shape, BF16),
            pltpu.VMEM((cell_dev, slots, half), BF16),
            pltpu.SMEM(cell_slot.shape, jnp.int32),
            pltpu.VMEM(probes.shape, jnp.int32),
            pltpu.VMEM(centroids.shape, F32),
            pltpu.SemaphoreType.DMA((peers,)),
            pltpu.SemaphoreType.DMA((peers,)),
            pltpu.SemaphoreType.DMA((pieces,)),
            pltpu.SemaphoreType.DMA((pieces,)),
            pltpu.SemaphoreType.DMA((pieces,)),
            pltpu.SemaphoreType.DMA((pieces,)),
            pltpu.SemaphoreType.DMA((2,)),
            pltpu.SemaphoreType.DMA((6,)),
        ],
        compiler_params=pltpu.CompilerParams(
            collective_id=0, has_side_effects=True, vmem_limit_bytes=64 << 20
        ),
    )(cell_slot, queries, probes, centroids, rotations, codebooks)

    group = 16
    groups = 2 * half_m // group
    table = pl.pallas_call(
        table_kernel,
        name="tables",
        grid=(cell_dev, groups),
        out_shape=jax.ShapeDtypeStruct(
            (owners, cell_dev, most, 2 * half_m, words), BF16
        ),
        in_specs=[
            pl.BlockSpec((1, slots, group * width), lambda l, m: (l, 0, m)),
            pl.BlockSpec((1, group, width, words), lambda l, m: (l, m, 0, 0)),
            pl.BlockSpec((1, slots, LANES), lambda l, m: (l, 0, 0)),
        ],
        out_specs=pl.BlockSpec(
            (owners, 1, most, group, words), lambda l, m: (0, l, 0, m, 0)
        ),
        compiler_params=pltpu.CompilerParams(vmem_limit_bytes=32 << 20),
    )(x, books, marks)
    return table.reshape(1, 1, owners * cell_dev * most, 2 * half_m, words)


def subspace_tables(rotated, books):
    width = books.shape[2]
    parts = rotated.reshape(rotated.shape[:-1] + (books.shape[1], width))
    cross = jnp.einsum("...lsmt,lmtk->...lsmk", parts, books, preferred_element_type=F32)
    wide = parts.astype(F32)
    own = jnp.sum(wide * wide, axis=-1)
    word = jnp.sum(jnp.square(books.astype(F32)), axis=2)
    return (own[..., None] - 2.0 * cross + word[:, None, :, :]) / width


def any_narrow(queries, probes, cell_slot, centroids, rotations, codebooks):
    q_dev, probe_count = probes.shape
    cells_all = cell_slot.shape[0]
    cell_dev = centroids.shape[0]
    depth = queries.shape[1]
    most = most_of(q_dev, probe_count, cells_all)
    owners = lax.axis_size("cells")
    span = jnp.arange(cells_all, dtype=jnp.int32)
    owner_hot = (cell_slot[:, None] == span[None, :]).astype(jnp.int32)
    probe_hot = (probes.reshape(-1)[:, None] == span[None, :]).astype(jnp.int32)
    position_hot = jnp.dot(probe_hot, owner_hot)
    rank = jnp.sum((jnp.cumsum(position_hot, axis=0) - position_hot) * position_hot, axis=1)
    position = jnp.dot(position_hot, span)
    slot = position * most + rank
    slot_span = jnp.arange(cells_all * most, dtype=jnp.int32)
    assign = jnp.sum(
        (slot[:, None] == slot_span[None, :])
        .astype(jnp.int32)
        .reshape(q_dev, probe_count, cells_all * most),
        axis=1,
    )
    send = jnp.einsum(
        "qs,qd->sd", assign.astype(BF16), queries, preferred_element_type=F32
    ).astype(BF16)
    valid = jnp.sum(assign, axis=0).astype(BF16)
    rows = lax.all_to_all(
        send.reshape(owners, cell_dev * most, depth), "cells", split_axis=0, concat_axis=0, tiled=True
    ).reshape(owners, cell_dev, most, depth)
    marks = lax.all_to_all(
        valid.reshape(owners, cell_dev * most), "cells", split_axis=0, concat_axis=0, tiled=True
    ).reshape(owners, cell_dev, most)
    residual = (rows.astype(F32) - centroids[None, :, None, :]).astype(BF16)
    rotated = jnp.einsum(
        "nilsd,lde->nilse",
        lax.all_gather(residual[None], "narrow", axis=0, tiled=True),
        rotations,
        preferred_element_type=F32,
    ).astype(BF16)
    gathered = subspace_tables(rotated, codebooks).astype(BF16)
    mine = lax.all_to_all(gathered, "narrow", split_axis=0, concat_axis=4, tiled=True)[0]
    table = mine * marks[..., None, None]
    return table.reshape((1, 1, owners * cell_dev * most) + table.shape[-2:])


def solution(mesh):
    return jax.shard_map(
        two_narrow if mesh.shape["narrow"] == mesh.shape["groups"] == 2 else any_narrow,
        mesh=mesh,
        in_specs=(
            P(("groups", "cells", "narrow"), None),
            P(("groups", "cells", "narrow"), None),
            P(),
            P("cells", None),
            P("cells", None, "narrow"),
            P("cells", "narrow", None, None),
        ),
        out_specs=P(("groups", "cells"), "narrow", None, None, None),
        check_vma=False,
    )
```

```python
import functools

import jax
import jax.numpy as jnp
from jax import lax
from jax.experimental import pallas as pl
from jax.experimental.pallas import tpu as pltpu
from jax.sharding import PartitionSpec as P

MESH = pl.DeviceIdType.MESH
F32 = jnp.float32
BF16 = jnp.bfloat16
LANES = 128
TABLE_STEPS = 2


def most_of(q_dev, probe_count, cells_all):
    return min(q_dev, max(2, 2 * q_dev * probe_count // cells_all))


def exchange_kernel(
    owners, most, slot_hbm, queries_hbm, probes_hbm, centroids_hbm, rotations, books,
    x_out, books_out, marks_out,
    blocks, turn, x_send, slot_of, probes, centroids,
    q_send_sem, q_recv_sem, b_send_sem, b_recv_sem, y_send_sem, y_recv_sem, r_sem, local_sem,
):
    q_dev, depth = queries_hbm.shape
    probe_count = probes.shape[1]
    cell_dev, half_m = books.shape[:2]
    half = rotations.shape[2]
    cells_all = slot_of.shape[0]
    rows = owners * q_dev
    slots = owners * most
    pieces = b_send_sem.shape[0]
    step = half_m // pieces
    g = lax.axis_index("groups")
    j = lax.axis_index("cells")
    n = lax.axis_index("narrow")
    other = 1 - n

    peers = [(dj, dn) for dn in (1, 0) for dj in range(owners) if (dj, dn) != (0, 0)]

    def target(dj, dn):
        return (g, lax.rem(j + dj, owners), lax.rem(n + dn, 2))

    across = (1 - g, j, n)
    barrier = pltpu.get_barrier_semaphore()
    for dj, dn in peers:
        pl.semaphore_signal(barrier, inc=1, device_id=target(dj, dn), device_id_type=MESH)
    pl.semaphore_signal(barrier, inc=1, device_id=across, device_id_type=MESH)

    loads = [
        pltpu.make_async_copy(src, dst, local_sem.at[i])
        for i, (src, dst) in enumerate(
            [
                (queries_hbm, blocks.at[n, j, :, pl.ds(0, depth)]),
                (probes_hbm, probes),
                (slot_hbm, slot_of),
                (centroids_hbm, centroids),
                (rotations, turn),
            ]
        )
    ]
    for load in loads:
        load.start()
    loads[1].wait()
    tail = jnp.concatenate(
        [probes[...].astype(F32), jnp.zeros((q_dev, LANES - probe_count), F32)], axis=1
    )
    blocks[n, j, :, depth:] = tail.astype(BF16)
    loads[0].wait()
    pl.semaphore_wait(barrier, len(peers) + 1)

    sends = []
    for k, (dj, dn) in enumerate(peers):
        copy = pltpu.make_async_remote_copy(
            src_ref=blocks.at[n, j],
            dst_ref=blocks.at[n, j],
            send_sem=q_send_sem.at[k],
            recv_sem=q_recv_sem.at[k],
            device_id=target(dj, dn),
            device_id_type=MESH,
        )
        copy.start()
        sends.append(copy)
    firsts = []
    for p in range(pieces):
        copy = pltpu.make_async_remote_copy(
            src_ref=books.at[g, pl.ds(p * step, step)],
            dst_ref=books_out.at[g, pl.ds(p * step, step)],
            send_sem=b_send_sem.at[p],
            recv_sem=b_recv_sem.at[p],
            device_id=(g, j, other),
            device_id_type=MESH,
        )
        copy.start()
        firsts.append(copy)
    relays = []

    def relay(p):
        firsts[p].wait_recv()
        piece = books_out.at[g, pl.ds(p * step, step)]
        copy = pltpu.make_async_remote_copy(
            src_ref=piece,
            dst_ref=piece,
            send_sem=y_send_sem.at[p],
            recv_sem=y_recv_sem.at[p],
            device_id=across,
            device_id_type=MESH,
        )
        copy.start()
        relays.append(copy)

    def arrived(dn):
        for k, (dj, kn) in enumerate(peers):
            if kn == dn:
                source = blocks.at[lax.rem(n + 2 - dn, 2), lax.rem(j + owners - dj, owners)]
                pltpu.make_async_remote_copy(
                    src_ref=source,
                    dst_ref=source,
                    send_sem=q_send_sem.at[k],
                    recv_sem=q_recv_sem.at[k],
                    device_id=target(dj, dn),
                    device_id_type=MESH,
                ).wait_recv()

    row = lax.broadcasted_iota(jnp.int32, (rows, rows), 0)
    col = lax.broadcasted_iota(jnp.int32, (rows, rows), 1)
    earlier = ((row < col) & (row // q_dev == col // q_dev)).astype(F32).astype(BF16)
    slot_row = lax.broadcasted_iota(jnp.int32, (slots, rows), 0)
    slot_col = lax.broadcasted_iota(jnp.int32, (slots, rows), 1)
    same = (slot_row // most == slot_col // q_dev).astype(F32)
    place = (slot_row % most).astype(F32)

    def cell_at(position):
        cell = jnp.int32(0)
        for c in range(cells_all):
            cell = cell + jnp.where(slot_of[c] == position, c, 0)
        return cell

    loads[2].wait()
    loads[3].wait()
    cells = [cell_at(j * cell_dev + l).astype(F32) for l in range(cell_dev)]

    def column(which):
        wide = blocks[which].astype(F32).reshape(rows, depth + LANES)
        named = wide[:, depth:]
        lane = lax.broadcasted_iota(jnp.int32, (rows, LANES), 1) < probe_count
        out = []
        for l in range(cell_dev):
            hit = ((named == cells[l]) & lane).astype(F32).astype(BF16)
            hits = lax.dot_general(
                jnp.ones((8, LANES), BF16), hit, (((1,), (1,)), ((), ())),
                preferred_element_type=F32,
            )
            rank = jnp.dot(hits.astype(BF16), earlier, preferred_element_type=F32)
            pick = (place == rank[:1]).astype(F32) * hits[:1] * same
            residual = (wide[:, :depth] - centroids[l : l + 1]).astype(BF16)
            rotated = jnp.dot(residual, turn[l], preferred_element_type=F32).astype(BF16)
            x = jnp.dot(pick.astype(BF16), rotated, preferred_element_type=F32).astype(BF16)
            out.append((x, pick))
        return out

    here = pl.ds(pl.multiple_of(n * half, LANES), half)
    for p in range(pieces // 2):
        relay(p)
    loads[4].wait()
    arrived(1)
    for l, (x, _) in enumerate(column(other)):
        x_send[l] = x
    x_copy = pltpu.make_async_remote_copy(
        src_ref=x_send,
        dst_ref=x_out.at[:, :, here],
        send_sem=r_sem.at[0],
        recv_sem=r_sem.at[1],
        device_id=(g, j, other),
        device_id_type=MESH,
    )
    x_copy.start()
    for p in range(pieces // 2, pieces):
        relay(p)
    arrived(0)
    for l, (x, pick) in enumerate(column(n)):
        x_out[l, :, here] = x
        marks_out[l] = jnp.broadcast_to(
            jnp.sum(pick, axis=1, keepdims=True), marks_out.shape[1:]
        )
    for copy in sends + firsts:
        copy.wait_send()
    x_copy.wait()
    for copy in relays:
        copy.wait()


def split3(value):
    high = value.astype(BF16)
    rest = value - high.astype(F32)
    middle = rest.astype(BF16)
    low = (rest - middle.astype(F32)).astype(BF16)
    return high, middle, low


def table_kernel(x_ref, own_ref, far_ref, marks_ref, out_ref):
    _, half_m, width, words = own_ref.shape
    slots = x_ref.shape[1]
    blocks, _, most = out_ref.shape[:3]
    group = 16
    span = group * width
    scale = 1.0 / width
    extra = LANES
    third = 3 * group
    n = lax.axis_index("narrow")

    lane = lax.broadcasted_iota(jnp.int32, (group, span + extra), 1)
    row = lax.broadcasted_iota(jnp.int32, (group, span + extra), 0)
    mask = (jnp.where(lane < span, lane // width, lane % group) == row).astype(F32)
    at = lax.broadcasted_iota(jnp.int32, (span, extra), 0) // width
    to = lax.broadcasted_iota(jnp.int32, (span, extra), 1)
    gather = ((to % group == at) & (to >= third) & (to < 2 * third)).astype(F32)
    gather = gather.astype(BF16)
    spot = lax.broadcasted_iota(jnp.int32, (slots, extra), 1)
    constant = [
        jnp.ones((third, words), BF16),
        jnp.zeros((extra - 2 * third, words), BF16),
    ]

    for books_ref, which in ((own_ref, n), (far_ref, 1 - n)):
        for piece in range(half_m // group):
            start = which * half_m + piece * group
            books = books_ref[0, piece * group : (piece + 1) * group]
            wide = books.astype(F32)
            word = jnp.sum(wide * wide, axis=1) * scale
            book = jnp.concatenate([books.reshape(span, words), *split3(word), *constant], axis=0)
            x = x_ref[0, :, pl.ds(pl.multiple_of(start * width, span), span)].astype(F32)
            square = x * x
            high = square.astype(BF16)
            low = (square - high.astype(F32)).astype(BF16)
            own = scale * (
                jnp.dot(high, gather, preferred_element_type=F32)
                + jnp.dot(low, gather, preferred_element_type=F32)
            )
            tops = [part.astype(F32) for part in split3(own)]
            part = jnp.where(
                spot < third + group,
                tops[0],
                jnp.where(spot < third + 2 * group, tops[1], tops[2]),
            )
            part = jnp.where(spot < third, marks_ref[0], part)
            left = jnp.concatenate([x * (-2.0 * scale), part], axis=1)
            spread = (left[:, None, :] * mask[None]).astype(BF16)
            table = jnp.dot(
                spread.reshape(slots * group, span + extra), book, preferred_element_type=F32
            )
            out_ref[:, :, :, pl.ds(pl.multiple_of(start, group), group), :] = table.astype(
                BF16
            ).reshape(blocks, 1, most, group, words)


def two_narrow(queries, probes, cell_slot, centroids, rotations, codebooks):
    q_dev, probe_count = probes.shape
    cells_all = cell_slot.shape[0]
    cell_dev, half_m, width, words = codebooks.shape
    depth = queries.shape[1]
    half = rotations.shape[2]
    owners = lax.axis_size("cells")
    most = most_of(q_dev, probe_count, cells_all)
    slots = owners * most
    peers = 2 * owners - 1
    vmem = pl.BlockSpec(memory_space=pltpu.VMEM)
    pieces = 4
    x, books, marks = pl.pallas_call(
        functools.partial(exchange_kernel, owners, most),
        name="exchange",
        out_shape=(
            jax.ShapeDtypeStruct((cell_dev, slots, depth), BF16),
            jax.ShapeDtypeStruct(codebooks.shape, BF16),
            jax.ShapeDtypeStruct((cell_dev, slots, LANES), F32),
        ),
        in_specs=[pl.BlockSpec(memory_space=pltpu.HBM)] * 6,
        out_specs=(vmem, pl.BlockSpec(memory_space=pl.ANY), vmem),
        scratch_shapes=[
            pltpu.VMEM((2, owners, q_dev, depth + LANES), BF16),
            pltpu.VMEM(rotations.shape, BF16),
            pltpu.VMEM((cell_dev, slots, half), BF16),
            pltpu.SMEM(cell_slot.shape, jnp.int32),
            pltpu.VMEM(probes.shape, jnp.int32),
            pltpu.VMEM(centroids.shape, F32),
            pltpu.SemaphoreType.DMA((peers,)),
            pltpu.SemaphoreType.DMA((peers,)),
            pltpu.SemaphoreType.DMA((pieces,)),
            pltpu.SemaphoreType.DMA((pieces,)),
            pltpu.SemaphoreType.DMA((pieces,)),
            pltpu.SemaphoreType.DMA((pieces,)),
            pltpu.SemaphoreType.DMA((2,)),
            pltpu.SemaphoreType.DMA((5,)),
        ],
        compiler_params=pltpu.CompilerParams(
            collective_id=0, has_side_effects=True, vmem_limit_bytes=64 << 20
        ),
    )(cell_slot, queries, probes, centroids, rotations, codebooks)

    part = max(owners // TABLE_STEPS, 1)
    table = pl.pallas_call(
        table_kernel,
        name="tables",
        grid=(cell_dev, owners // part),
        out_shape=jax.ShapeDtypeStruct((owners, cell_dev, most, 2 * half_m, words), BF16),
        in_specs=[
            pl.BlockSpec((1, part * most, depth), lambda l, i: (l, i, 0)),
            pl.BlockSpec((1, half_m, width, words), lambda l, i: (l, 0, 0, 0)),
            pl.BlockSpec((1, half_m, width, words), lambda l, i: (l, 0, 0, 0)),
            pl.BlockSpec((1, part * most, LANES), lambda l, i: (l, i, 0)),
        ],
        out_specs=pl.BlockSpec(
            (part, 1, most, 2 * half_m, words), lambda l, i: (i, l, 0, 0, 0)
        ),
        compiler_params=pltpu.CompilerParams(vmem_limit_bytes=64 << 20),
    )(x, codebooks, books, marks)
    return table.reshape(1, 1, owners * cell_dev * most, 2 * half_m, words)


def subspace_tables(rotated, books):
    width = books.shape[2]
    parts = rotated.reshape(rotated.shape[:-1] + (books.shape[1], width))
    cross = jnp.einsum("...lsmt,lmtk->...lsmk", parts, books, preferred_element_type=F32)
    wide = parts.astype(F32)
    own = jnp.sum(wide * wide, axis=-1)
    word = jnp.sum(jnp.square(books.astype(F32)), axis=2)
    return (own[..., None] - 2.0 * cross + word[:, None, :, :]) / width


def any_narrow(queries, probes, cell_slot, centroids, rotations, codebooks):
    q_dev, probe_count = probes.shape
    cells_all = cell_slot.shape[0]
    cell_dev = centroids.shape[0]
    depth = queries.shape[1]
    most = most_of(q_dev, probe_count, cells_all)
    owners = lax.axis_size("cells")
    span = jnp.arange(cells_all, dtype=jnp.int32)
    owner_hot = (cell_slot[:, None] == span[None, :]).astype(jnp.int32)
    probe_hot = (probes.reshape(-1)[:, None] == span[None, :]).astype(jnp.int32)
    position_hot = jnp.dot(probe_hot, owner_hot)
    rank = jnp.sum((jnp.cumsum(position_hot, axis=0) - position_hot) * position_hot, axis=1)
    position = jnp.dot(position_hot, span)
    slot = position * most + rank
    slot_span = jnp.arange(cells_all * most, dtype=jnp.int32)
    assign = jnp.sum(
        (slot[:, None] == slot_span[None, :])
        .astype(jnp.int32)
        .reshape(q_dev, probe_count, cells_all * most),
        axis=1,
    )
    send = jnp.einsum(
        "qs,qd->sd", assign.astype(BF16), queries, preferred_element_type=F32
    ).astype(BF16)
    valid = jnp.sum(assign, axis=0).astype(BF16)
    rows = lax.all_to_all(
        send.reshape(owners, cell_dev * most, depth), "cells", split_axis=0, concat_axis=0, tiled=True
    ).reshape(owners, cell_dev, most, depth)
    marks = lax.all_to_all(
        valid.reshape(owners, cell_dev * most), "cells", split_axis=0, concat_axis=0, tiled=True
    ).reshape(owners, cell_dev, most)
    residual = (rows.astype(F32) - centroids[None, :, None, :]).astype(BF16)
    rotated = jnp.einsum(
        "nilsd,lde->nilse",
        lax.all_gather(residual[None], "narrow", axis=0, tiled=True),
        rotations,
        preferred_element_type=F32,
    ).astype(BF16)
    gathered = subspace_tables(rotated, codebooks).astype(BF16)
    mine = lax.all_to_all(gathered, "narrow", split_axis=0, concat_axis=4, tiled=True)[0]
    table = mine * marks[..., None, None]
    return table.reshape((1, 1, owners * cell_dev * most) + table.shape[-2:])


def solution(mesh):
    return jax.shard_map(
        two_narrow if mesh.shape["narrow"] == mesh.shape["groups"] == 2 else any_narrow,
        mesh=mesh,
        in_specs=(
            P(("groups", "cells", "narrow"), None),
            P(("groups", "cells", "narrow"), None),
            P(),
            P("cells", None),
            P("cells", None, "narrow"),
            P("cells", "narrow", None, None),
        ),
        out_specs=P(("groups", "cells"), "narrow", None, None, None),
        check_vma=False,
    )
```

```python
import functools

import jax
import jax.numpy as jnp
from jax import lax
from jax.experimental import pallas as pl
from jax.experimental.pallas import tpu as pltpu
from jax.sharding import PartitionSpec as P

MESH = pl.DeviceIdType.MESH
F32 = jnp.float32
BF16 = jnp.bfloat16
LANES = 128
TABLE_STEPS = 1


def most_of(q_dev, probe_count, cells_all):
    return min(q_dev, max(2, 2 * q_dev * probe_count // cells_all))


def exchange_kernel(
    owners, most, slot_hbm, queries_hbm, probes_hbm, centroids_hbm, rotations, books,
    x_out, books_out, marks_out,
    blocks, turn, x_send, slot_of, probes, centroids,
    q_send_sem, q_recv_sem, b_send_sem, b_recv_sem, y_send_sem, y_recv_sem, x_send_sem, x_recv_sem, local_sem,
):
    q_dev, depth = queries_hbm.shape
    probe_count = probes.shape[1]
    cell_dev, half_m = books.shape[:2]
    half = rotations.shape[2]
    cells_all = slot_of.shape[0]
    rows = owners * q_dev
    slots = owners * most
    pieces = b_send_sem.shape[0]
    step = half_m // pieces
    g = lax.axis_index("groups")
    j = lax.axis_index("cells")
    n = lax.axis_index("narrow")
    other = 1 - n

    hops = range(1, owners // 2)
    beside = j + 1 - 2 * lax.rem(j, 2)
    facing = (g, j, other)
    paired = (g, beside, n)

    def ahead(d):
        return (g, lax.rem(j + 2 * d, owners), n)

    def behind(cell, d):
        return lax.rem(cell + owners - 2 * d, owners)

    across = (1 - g, j, n)
    barrier = pltpu.get_barrier_semaphore()
    partners = [facing, paired, across] + [ahead(d) for d in hops]
    for partner in partners:
        pl.semaphore_signal(barrier, inc=1, device_id=partner, device_id_type=MESH)

    loads = [
        pltpu.make_async_copy(src, dst, local_sem.at[i])
        for i, (src, dst) in enumerate(
            [
                (queries_hbm, blocks.at[n, j, :, pl.ds(0, depth)]),
                (probes_hbm, probes),
                (slot_hbm, slot_of),
                (centroids_hbm, centroids),
                (rotations, turn),
            ]
        )
    ]
    for load in loads:
        load.start()
    loads[1].wait()
    tail = jnp.concatenate(
        [probes[...].astype(F32), jnp.zeros((q_dev, LANES - probe_count), F32)], axis=1
    )
    blocks[n, j, :, depth:] = tail.astype(BF16)
    loads[0].wait()
    pl.semaphore_wait(barrier, len(partners))

    def block_copy(k, column_at, cell, device):
        return pltpu.make_async_remote_copy(
            src_ref=blocks.at[column_at, cell],
            dst_ref=blocks.at[column_at, cell],
            send_sem=q_send_sem.at[k],
            recv_sem=q_recv_sem.at[k],
            device_id=device,
            device_id_type=MESH,
        )

    sends = []

    def send(k, column_at, cell, device):
        copy = block_copy(k, column_at, cell, device)
        copy.start()
        sends.append(copy)

    count = 2 * len(hops) + 1

    def from_behind(c, d):
        return 1 + c * count + d - 1

    def from_paired(c, d):
        return 1 + c * count + len(hops) + d

    columns = (n, other)
    send(0, n, j, facing)
    for d in hops:
        send(from_behind(0, d), n, j, ahead(d))
    send(from_paired(0, 0), n, j, paired)
    firsts = []
    for p in range(pieces):
        copy = pltpu.make_async_remote_copy(
            src_ref=books.at[g, pl.ds(p * step, step)],
            dst_ref=books_out.at[g, pl.ds(p * step, step)],
            send_sem=b_send_sem.at[p],
            recv_sem=b_recv_sem.at[p],
            device_id=(g, j, other),
            device_id_type=MESH,
        )
        copy.start()
        firsts.append(copy)
    relays = []

    def relay(p):
        firsts[p].wait_recv()
        piece = books_out.at[g, pl.ds(p * step, step)]
        copy = pltpu.make_async_remote_copy(
            src_ref=piece,
            dst_ref=piece,
            send_sem=y_send_sem.at[p],
            recv_sem=y_recv_sem.at[p],
            device_id=across,
            device_id_type=MESH,
        )
        copy.start()
        relays.append(copy)

    block_copy(0, other, j, facing).wait_recv()
    for d in hops:
        send(from_behind(1, d), other, j, ahead(d))
    send(from_paired(1, 0), other, j, paired)

    def pass_on(c):
        for d in hops:
            block_copy(from_behind(c, d), columns[c], behind(j, d), paired).wait_recv()
            send(from_paired(c, d), columns[c], behind(j, d), paired)

    def arrived(c):
        for d in range(owners // 2):
            block_copy(
                from_paired(c, d), columns[c], behind(beside, d), paired
            ).wait_recv()

    row = lax.broadcasted_iota(jnp.int32, (rows, rows), 0)
    col = lax.broadcasted_iota(jnp.int32, (rows, rows), 1)
    earlier = ((row < col) & (row // q_dev == col // q_dev)).astype(F32).astype(BF16)
    slot_row = lax.broadcasted_iota(jnp.int32, (slots, rows), 0)
    slot_col = lax.broadcasted_iota(jnp.int32, (slots, rows), 1)
    same = (slot_row // most == slot_col // q_dev).astype(F32)
    place = (slot_row % most).astype(F32)

    def cell_at(position):
        cell = jnp.int32(0)
        for c in range(cells_all):
            cell = cell + jnp.where(slot_of[c] == position, c, 0)
        return cell

    loads[2].wait()
    loads[3].wait()
    cells = [cell_at(j * cell_dev + l).astype(F32) for l in range(cell_dev)]

    def column(which):
        wide = blocks[which].astype(F32).reshape(rows, depth + LANES)
        named = wide[:, depth:]
        lane = lax.broadcasted_iota(jnp.int32, (rows, LANES), 1) < probe_count
        for l in range(cell_dev):
            hit = ((named == cells[l]) & lane).astype(F32).astype(BF16)
            hits = lax.dot_general(
                jnp.ones((8, LANES), BF16), hit, (((1,), (1,)), ((), ())),
                preferred_element_type=F32,
            )
            rank = jnp.dot(hits.astype(BF16), earlier, preferred_element_type=F32)
            pick = (place == rank[:1]).astype(F32) * hits[:1] * same
            residual = (wide[:, :depth] - centroids[l : l + 1]).astype(BF16)
            rotated = jnp.dot(residual, turn[l], preferred_element_type=F32).astype(BF16)
            x = jnp.dot(pick.astype(BF16), rotated, preferred_element_type=F32).astype(BF16)
            yield x, pick

    here = pl.ds(pl.multiple_of(n * half, LANES), half)
    relay(0)
    pass_on(1)
    pass_on(0)
    loads[4].wait()
    arrived(1)
    x_copies = []
    for l, (x, _) in enumerate(column(other)):
        x_send[l] = x
        copy = pltpu.make_async_remote_copy(
            src_ref=x_send.at[l],
            dst_ref=x_out.at[l, :, here],
            send_sem=x_send_sem.at[l],
            recv_sem=x_recv_sem.at[l],
            device_id=facing,
            device_id_type=MESH,
        )
        copy.start()
        x_copies.append(copy)
    for p in range(1, pieces):
        relay(p)
    arrived(0)
    for l, (x, pick) in enumerate(column(n)):
        x_out[l, :, here] = x
        marks_out[l] = jnp.broadcast_to(
            jnp.sum(pick, axis=1, keepdims=True), marks_out.shape[1:]
        )
    for copy in sends + firsts:
        copy.wait_send()
    for copy in x_copies + relays:
        copy.wait()


def split3(value):
    high = value.astype(BF16)
    rest = value - high.astype(F32)
    middle = rest.astype(BF16)
    low = (rest - middle.astype(F32)).astype(BF16)
    return high, middle, low


def table_kernel(x_ref, own_ref, far_ref, marks_ref, out_ref):
    _, half_m, width, words = own_ref.shape
    slots = x_ref.shape[1]
    blocks, _, most = out_ref.shape[:3]
    group = 16
    span = group * width
    scale = 1.0 / width
    extra = LANES
    third = 3 * group
    n = lax.axis_index("narrow")

    lane = lax.broadcasted_iota(jnp.int32, (group, span + extra), 1)
    row = lax.broadcasted_iota(jnp.int32, (group, span + extra), 0)
    mask = (jnp.where(lane < span, lane // width, lane % group) == row).astype(F32)
    at = lax.broadcasted_iota(jnp.int32, (span, extra), 0) // width
    to = lax.broadcasted_iota(jnp.int32, (span, extra), 1)
    gather = ((to % group == at) & (to >= third) & (to < 2 * third)).astype(F32)
    gather = gather.astype(BF16)
    spot = lax.broadcasted_iota(jnp.int32, (slots, extra), 1)
    constant = [
        jnp.ones((third, words), BF16),
        jnp.zeros((extra - 2 * third, words), BF16),
    ]

    for books_ref, which in ((own_ref, n), (far_ref, 1 - n)):
        for piece in range(half_m // group):
            start = which * half_m + piece * group
            books = books_ref[0, piece * group : (piece + 1) * group]
            wide = books.astype(F32)
            word = jnp.sum(wide * wide, axis=1) * scale
            book = jnp.concatenate([books.reshape(span, words), *split3(word), *constant], axis=0)
            x = x_ref[0, :, pl.ds(pl.multiple_of(start * width, span), span)].astype(F32)
            square = x * x
            high = square.astype(BF16)
            low = (square - high.astype(F32)).astype(BF16)
            own = scale * (
                jnp.dot(high, gather, preferred_element_type=F32)
                + jnp.dot(low, gather, preferred_element_type=F32)
            )
            tops = [part.astype(F32) for part in split3(own)]
            part = jnp.where(
                spot < third + group,
                tops[0],
                jnp.where(spot < third + 2 * group, tops[1], tops[2]),
            )
            part = jnp.where(spot < third, marks_ref[0], part)
            left = jnp.concatenate([x * (-2.0 * scale), part], axis=1)
            spread = (left[:, None, :] * mask[None]).astype(BF16)
            table = jnp.dot(
                spread.reshape(slots * group, span + extra), book, preferred_element_type=F32
            )
            out_ref[:, :, :, pl.ds(pl.multiple_of(start, group), group), :] = table.astype(
                BF16
            ).reshape(blocks, 1, most, group, words)


def two_narrow(queries, probes, cell_slot, centroids, rotations, codebooks):
    q_dev, probe_count = probes.shape
    cells_all = cell_slot.shape[0]
    cell_dev, half_m, width, words = codebooks.shape
    depth = queries.shape[1]
    half = rotations.shape[2]
    owners = lax.axis_size("cells")
    most = most_of(q_dev, probe_count, cells_all)
    slots = owners * most
    peers = 2 * owners - 1
    vmem = pl.BlockSpec(memory_space=pltpu.VMEM)
    pieces = 4
    x, books, marks = pl.pallas_call(
        functools.partial(exchange_kernel, owners, most),
        name="exchange",
        out_shape=(
            jax.ShapeDtypeStruct((cell_dev, slots, depth), BF16),
            jax.ShapeDtypeStruct(codebooks.shape, BF16),
            jax.ShapeDtypeStruct((cell_dev, slots, LANES), F32),
        ),
        in_specs=[pl.BlockSpec(memory_space=pltpu.HBM)] * 6,
        out_specs=(vmem, pl.BlockSpec(memory_space=pl.ANY), vmem),
        scratch_shapes=[
            pltpu.VMEM((2, owners, q_dev, depth + LANES), BF16),
            pltpu.VMEM(rotations.shape, BF16),
            pltpu.VMEM((cell_dev, slots, half), BF16),
            pltpu.SMEM(cell_slot.shape, jnp.int32),
            pltpu.VMEM(probes.shape, jnp.int32),
            pltpu.VMEM(centroids.shape, F32),
            pltpu.SemaphoreType.DMA((peers,)),
            pltpu.SemaphoreType.DMA((peers,)),
            pltpu.SemaphoreType.DMA((pieces,)),
            pltpu.SemaphoreType.DMA((pieces,)),
            pltpu.SemaphoreType.DMA((pieces,)),
            pltpu.SemaphoreType.DMA((pieces,)),
            pltpu.SemaphoreType.DMA((cell_dev,)),
            pltpu.SemaphoreType.DMA((cell_dev,)),
            pltpu.SemaphoreType.DMA((5,)),
        ],
        compiler_params=pltpu.CompilerParams(
            collective_id=0, has_side_effects=True, vmem_limit_bytes=64 << 20
        ),
    )(cell_slot, queries, probes, centroids, rotations, codebooks)

    part = max(owners // TABLE_STEPS, 1)
    table = pl.pallas_call(
        table_kernel,
        name="tables",
        grid=(cell_dev, owners // part),
        out_shape=jax.ShapeDtypeStruct((owners, cell_dev, most, 2 * half_m, words), BF16),
        in_specs=[
            pl.BlockSpec((1, part * most, depth), lambda l, i: (l, i, 0)),
            pl.BlockSpec((1, half_m, width, words), lambda l, i: (l, 0, 0, 0)),
            pl.BlockSpec((1, half_m, width, words), lambda l, i: (l, 0, 0, 0)),
            pl.BlockSpec((1, part * most, LANES), lambda l, i: (l, i, 0)),
        ],
        out_specs=pl.BlockSpec(
            (part, 1, most, 2 * half_m, words), lambda l, i: (i, l, 0, 0, 0)
        ),
        compiler_params=pltpu.CompilerParams(vmem_limit_bytes=64 << 20),
    )(x, codebooks, books, marks)
    return table.reshape(1, 1, owners * cell_dev * most, 2 * half_m, words)


def subspace_tables(rotated, books):
    width = books.shape[2]
    parts = rotated.reshape(rotated.shape[:-1] + (books.shape[1], width))
    cross = jnp.einsum("...lsmt,lmtk->...lsmk", parts, books, preferred_element_type=F32)
    wide = parts.astype(F32)
    own = jnp.sum(wide * wide, axis=-1)
    word = jnp.sum(jnp.square(books.astype(F32)), axis=2)
    return (own[..., None] - 2.0 * cross + word[:, None, :, :]) / width


def any_narrow(queries, probes, cell_slot, centroids, rotations, codebooks):
    q_dev, probe_count = probes.shape
    cells_all = cell_slot.shape[0]
    cell_dev = centroids.shape[0]
    depth = queries.shape[1]
    most = most_of(q_dev, probe_count, cells_all)
    owners = lax.axis_size("cells")
    span = jnp.arange(cells_all, dtype=jnp.int32)
    owner_hot = (cell_slot[:, None] == span[None, :]).astype(jnp.int32)
    probe_hot = (probes.reshape(-1)[:, None] == span[None, :]).astype(jnp.int32)
    position_hot = jnp.dot(probe_hot, owner_hot)
    rank = jnp.sum((jnp.cumsum(position_hot, axis=0) - position_hot) * position_hot, axis=1)
    position = jnp.dot(position_hot, span)
    slot = position * most + rank
    slot_span = jnp.arange(cells_all * most, dtype=jnp.int32)
    assign = jnp.sum(
        (slot[:, None] == slot_span[None, :])
        .astype(jnp.int32)
        .reshape(q_dev, probe_count, cells_all * most),
        axis=1,
    )
    send = jnp.einsum(
        "qs,qd->sd", assign.astype(BF16), queries, preferred_element_type=F32
    ).astype(BF16)
    valid = jnp.sum(assign, axis=0).astype(BF16)
    rows = lax.all_to_all(
        send.reshape(owners, cell_dev * most, depth), "cells", split_axis=0, concat_axis=0, tiled=True
    ).reshape(owners, cell_dev, most, depth)
    marks = lax.all_to_all(
        valid.reshape(owners, cell_dev * most), "cells", split_axis=0, concat_axis=0, tiled=True
    ).reshape(owners, cell_dev, most)
    residual = (rows.astype(F32) - centroids[None, :, None, :]).astype(BF16)
    rotated = jnp.einsum(
        "nilsd,lde->nilse",
        lax.all_gather(residual[None], "narrow", axis=0, tiled=True),
        rotations,
        preferred_element_type=F32,
    ).astype(BF16)
    gathered = subspace_tables(rotated, codebooks).astype(BF16)
    mine = lax.all_to_all(gathered, "narrow", split_axis=0, concat_axis=4, tiled=True)[0]
    table = mine * marks[..., None, None]
    return table.reshape((1, 1, owners * cell_dev * most) + table.shape[-2:])


def solution(mesh):
    return jax.shard_map(
        two_narrow if mesh.shape["narrow"] == mesh.shape["groups"] == 2 and mesh.shape["cells"] % 2 == 0 else any_narrow,
        mesh=mesh,
        in_specs=(
            P(("groups", "cells", "narrow"), None),
            P(("groups", "cells", "narrow"), None),
            P(),
            P("cells", None),
            P("cells", None, "narrow"),
            P("cells", "narrow", None, None),
        ),
        out_specs=P(("groups", "cells"), "narrow", None, None, None),
        check_vma=False,
    )
```

```python
import functools

import jax
import jax.numpy as jnp
from jax import lax
from jax.experimental import pallas as pl
from jax.experimental.pallas import tpu as pltpu
from jax.sharding import PartitionSpec as P

MESH = pl.DeviceIdType.MESH
F32 = jnp.float32
BF16 = jnp.bfloat16
LANES = 128
TABLE_STEPS = 1


def most_of(q_dev, probe_count, cells_all):
    return min(q_dev, max(2, 2 * q_dev * probe_count // cells_all))


def exchange_kernel(
    owners, most, slot_hbm, queries_hbm, probes_hbm, centroids_hbm, rotations, books,
    x_out, books_out, marks_out,
    blocks, turn, x_send, slot_of, probes, centroids,
    q_send_sem, q_recv_sem, b_send_sem, b_recv_sem, y_send_sem, y_recv_sem, x_send_sem, x_recv_sem, local_sem,
):
    q_dev, depth = queries_hbm.shape
    probe_count = probes.shape[1]
    cell_dev, half_m = books.shape[:2]
    half = rotations.shape[2]
    cells_all = slot_of.shape[0]
    rows = owners * q_dev
    slots = owners * most
    pieces = b_send_sem.shape[0]
    step = half_m // pieces
    g = lax.axis_index("groups")
    j = lax.axis_index("cells")
    n = lax.axis_index("narrow")
    other = 1 - n

    hops = range(1, owners // 2)
    beside = j + 1 - 2 * lax.rem(j, 2)
    facing = (g, j, other)
    paired = (g, beside, n)

    def ahead(d):
        return (g, lax.rem(j + 2 * d, owners), n)

    def behind(cell, d):
        return lax.rem(cell + owners - 2 * d, owners)

    across = (1 - g, j, n)
    barrier = pltpu.get_barrier_semaphore()
    partners = [facing, paired, across] + [ahead(d) for d in hops]
    for partner in partners:
        pl.semaphore_signal(barrier, inc=1, device_id=partner, device_id_type=MESH)

    loads = [
        pltpu.make_async_copy(src, dst, local_sem.at[i])
        for i, (src, dst) in enumerate(
            [
                (queries_hbm, blocks.at[n, j, :, pl.ds(0, depth)]),
                (probes_hbm, probes),
                (slot_hbm, slot_of),
                (centroids_hbm, centroids),
                (rotations, turn),
            ]
        )
    ]
    for load in loads:
        load.start()
    loads[1].wait()
    tail = jnp.concatenate(
        [probes[...].astype(F32), jnp.zeros((q_dev, LANES - probe_count), F32)], axis=1
    )
    blocks[n, j, :, depth:] = tail.astype(BF16)
    loads[0].wait()
    pl.semaphore_wait(barrier, len(partners))

    def block_copy(k, column_at, cell, device):
        return pltpu.make_async_remote_copy(
            src_ref=blocks.at[column_at, cell],
            dst_ref=blocks.at[column_at, cell],
            send_sem=q_send_sem.at[k],
            recv_sem=q_recv_sem.at[k],
            device_id=device,
            device_id_type=MESH,
        )

    sends = []

    def send(k, column_at, cell, device):
        copy = block_copy(k, column_at, cell, device)
        copy.start()
        sends.append(copy)

    count = 2 * len(hops) + 1

    def from_behind(c, d):
        return 1 + c * count + d - 1

    def from_paired(c, d):
        return 1 + c * count + len(hops) + d

    columns = (n, other)
    send(0, n, j, facing)
    for d in hops:
        send(from_behind(0, d), n, j, ahead(d))
    send(from_paired(0, 0), n, j, paired)
    firsts = []
    for p in range(pieces):
        copy = pltpu.make_async_remote_copy(
            src_ref=books.at[g, pl.ds(p * step, step)],
            dst_ref=books_out.at[g, pl.ds(p * step, step)],
            send_sem=b_send_sem.at[p],
            recv_sem=b_recv_sem.at[p],
            device_id=(g, j, other),
            device_id_type=MESH,
        )
        copy.start()
        firsts.append(copy)
    relays = []

    def relay(p):
        firsts[p].wait_recv()
        piece = books_out.at[g, pl.ds(p * step, step)]
        copy = pltpu.make_async_remote_copy(
            src_ref=piece,
            dst_ref=piece,
            send_sem=y_send_sem.at[p],
            recv_sem=y_recv_sem.at[p],
            device_id=across,
            device_id_type=MESH,
        )
        copy.start()
        relays.append(copy)

    block_copy(0, other, j, facing).wait_recv()
    for d in hops:
        send(from_behind(1, d), other, j, ahead(d))
    send(from_paired(1, 0), other, j, paired)

    def pass_on(c):
        for d in hops:
            block_copy(from_behind(c, d), columns[c], behind(j, d), paired).wait_recv()
            send(from_paired(c, d), columns[c], behind(j, d), paired)

    def arrived(c):
        for d in range(owners // 2):
            block_copy(
                from_paired(c, d), columns[c], behind(beside, d), paired
            ).wait_recv()

    row = lax.broadcasted_iota(jnp.int32, (rows, rows), 0)
    col = lax.broadcasted_iota(jnp.int32, (rows, rows), 1)
    earlier = ((row < col) & (row // q_dev == col // q_dev)).astype(F32).astype(BF16)
    slot_row = lax.broadcasted_iota(jnp.int32, (slots, rows), 0)
    slot_col = lax.broadcasted_iota(jnp.int32, (slots, rows), 1)
    same = (slot_row // most == slot_col // q_dev).astype(F32)
    place = (slot_row % most).astype(F32)

    def cell_at(position):
        cell = jnp.int32(0)
        for c in range(cells_all):
            cell = cell + jnp.where(slot_of[c] == position, c, 0)
        return cell

    loads[2].wait()
    loads[3].wait()
    cells = [cell_at(j * cell_dev + l).astype(F32) for l in range(cell_dev)]

    def column(which):
        wide = blocks[which].astype(F32).reshape(rows, depth + LANES)
        named = wide[:, depth:]
        lane = lax.broadcasted_iota(jnp.int32, (rows, LANES), 1) < probe_count
        for l in range(cell_dev):
            hit = ((named == cells[l]) & lane).astype(F32).astype(BF16)
            hits = lax.dot_general(
                jnp.ones((8, LANES), BF16), hit, (((1,), (1,)), ((), ())),
                preferred_element_type=F32,
            )
            rank = jnp.dot(hits.astype(BF16), earlier, preferred_element_type=F32)
            pick = (place == rank[:1]).astype(F32) * hits[:1] * same
            residual = (wide[:, :depth] - centroids[l : l + 1]).astype(BF16)
            rotated = jnp.dot(residual, turn[l], preferred_element_type=F32).astype(BF16)
            x = jnp.dot(pick.astype(BF16), rotated, preferred_element_type=F32).astype(BF16)
            yield x, pick

    here = pl.ds(pl.multiple_of(n * half, LANES), half)
    relay(0)
    pass_on(1)
    relay(1)
    pass_on(0)
    for p in range(2, pieces - 1):
        relay(p)
    loads[4].wait()
    arrived(1)
    relay(pieces - 1)
    x_copies = []
    for l, (x, _) in enumerate(column(other)):
        x_send[l] = x
        copy = pltpu.make_async_remote_copy(
            src_ref=x_send.at[l],
            dst_ref=x_out.at[l, :, here],
            send_sem=x_send_sem.at[l],
            recv_sem=x_recv_sem.at[l],
            device_id=facing,
            device_id_type=MESH,
        )
        copy.start()
        x_copies.append(copy)
    arrived(0)
    for l, (x, pick) in enumerate(column(n)):
        x_out[l, :, here] = x
        marks_out[l] = jnp.broadcast_to(
            jnp.sum(pick, axis=1, keepdims=True), marks_out.shape[1:]
        )
    for copy in sends + firsts:
        copy.wait_send()
    for copy in x_copies + relays:
        copy.wait()


def split3(value):
    high = value.astype(BF16)
    rest = value - high.astype(F32)
    middle = rest.astype(BF16)
    low = (rest - middle.astype(F32)).astype(BF16)
    return high, middle, low


def table_kernel(x_ref, own_ref, far_ref, marks_ref, out_ref):
    _, half_m, width, words = own_ref.shape
    slots = x_ref.shape[1]
    blocks, _, most = out_ref.shape[:3]
    group = 16
    span = group * width
    scale = 1.0 / width
    extra = LANES
    third = 3 * group
    n = lax.axis_index("narrow")

    lane = lax.broadcasted_iota(jnp.int32, (group, span + extra), 1)
    row = lax.broadcasted_iota(jnp.int32, (group, span + extra), 0)
    mask = (jnp.where(lane < span, lane // width, lane % group) == row).astype(F32)
    at = lax.broadcasted_iota(jnp.int32, (span, extra), 0) // width
    to = lax.broadcasted_iota(jnp.int32, (span, extra), 1)
    gather = ((to % group == at) & (to >= third) & (to < 2 * third)).astype(F32)
    gather = gather.astype(BF16)
    spot = lax.broadcasted_iota(jnp.int32, (slots, extra), 1)
    constant = [
        jnp.ones((third, words), BF16),
        jnp.zeros((extra - 2 * third, words), BF16),
    ]

    for books_ref, which in ((own_ref, n), (far_ref, 1 - n)):
        for piece in range(half_m // group):
            start = which * half_m + piece * group
            books = books_ref[0, piece * group : (piece + 1) * group]
            wide = books.astype(F32)
            word = jnp.sum(wide * wide, axis=1) * scale
            book = jnp.concatenate([books.reshape(span, words), *split3(word), *constant], axis=0)
            x = x_ref[0, :, pl.ds(pl.multiple_of(start * width, span), span)].astype(F32)
            square = x * x
            high = square.astype(BF16)
            low = (square - high.astype(F32)).astype(BF16)
            own = scale * (
                jnp.dot(high, gather, preferred_element_type=F32)
                + jnp.dot(low, gather, preferred_element_type=F32)
            )
            tops = [part.astype(F32) for part in split3(own)]
            part = jnp.where(
                spot < third + group,
                tops[0],
                jnp.where(spot < third + 2 * group, tops[1], tops[2]),
            )
            part = jnp.where(spot < third, marks_ref[0], part)
            left = jnp.concatenate([x * (-2.0 * scale), part], axis=1)
            spread = (left[:, None, :] * mask[None]).astype(BF16)
            table = jnp.dot(
                spread.reshape(slots * group, span + extra), book, preferred_element_type=F32
            )
            out_ref[:, :, :, pl.ds(pl.multiple_of(start, group), group), :] = table.astype(
                BF16
            ).reshape(blocks, 1, most, group, words)


def two_narrow(queries, probes, cell_slot, centroids, rotations, codebooks):
    q_dev, probe_count = probes.shape
    cells_all = cell_slot.shape[0]
    cell_dev, half_m, width, words = codebooks.shape
    depth = queries.shape[1]
    half = rotations.shape[2]
    owners = lax.axis_size("cells")
    most = most_of(q_dev, probe_count, cells_all)
    slots = owners * most
    peers = 2 * owners - 1
    vmem = pl.BlockSpec(memory_space=pltpu.VMEM)
    pieces = 4
    x, books, marks = pl.pallas_call(
        functools.partial(exchange_kernel, owners, most),
        name="exchange",
        out_shape=(
            jax.ShapeDtypeStruct((cell_dev, slots, depth), BF16),
            jax.ShapeDtypeStruct(codebooks.shape, BF16),
            jax.ShapeDtypeStruct((cell_dev, slots, LANES), F32),
        ),
        in_specs=[pl.BlockSpec(memory_space=pltpu.HBM)] * 6,
        out_specs=(vmem, pl.BlockSpec(memory_space=pl.ANY), vmem),
        scratch_shapes=[
            pltpu.VMEM((2, owners, q_dev, depth + LANES), BF16),
            pltpu.VMEM(rotations.shape, BF16),
            pltpu.VMEM((cell_dev, slots, half), BF16),
            pltpu.SMEM(cell_slot.shape, jnp.int32),
            pltpu.VMEM(probes.shape, jnp.int32),
            pltpu.VMEM(centroids.shape, F32),
            pltpu.SemaphoreType.DMA((peers,)),
            pltpu.SemaphoreType.DMA((peers,)),
            pltpu.SemaphoreType.DMA((pieces,)),
            pltpu.SemaphoreType.DMA((pieces,)),
            pltpu.SemaphoreType.DMA((pieces,)),
            pltpu.SemaphoreType.DMA((pieces,)),
            pltpu.SemaphoreType.DMA((cell_dev,)),
            pltpu.SemaphoreType.DMA((cell_dev,)),
            pltpu.SemaphoreType.DMA((5,)),
        ],
        compiler_params=pltpu.CompilerParams(
            collective_id=0, has_side_effects=True, vmem_limit_bytes=64 << 20
        ),
    )(cell_slot, queries, probes, centroids, rotations, codebooks)

    part = max(owners // TABLE_STEPS, 1)
    table = pl.pallas_call(
        table_kernel,
        name="tables",
        grid=(cell_dev, owners // part),
        out_shape=jax.ShapeDtypeStruct((owners, cell_dev, most, 2 * half_m, words), BF16),
        in_specs=[
            pl.BlockSpec((1, part * most, depth), lambda l, i: (l, i, 0)),
            pl.BlockSpec((1, half_m, width, words), lambda l, i: (l, 0, 0, 0)),
            pl.BlockSpec((1, half_m, width, words), lambda l, i: (l, 0, 0, 0)),
            pl.BlockSpec((1, part * most, LANES), lambda l, i: (l, i, 0)),
        ],
        out_specs=pl.BlockSpec(
            (part, 1, most, 2 * half_m, words), lambda l, i: (i, l, 0, 0, 0)
        ),
        compiler_params=pltpu.CompilerParams(vmem_limit_bytes=64 << 20),
    )(x, codebooks, books, marks)
    return table.reshape(1, 1, owners * cell_dev * most, 2 * half_m, words)


def subspace_tables(rotated, books):
    width = books.shape[2]
    parts = rotated.reshape(rotated.shape[:-1] + (books.shape[1], width))
    cross = jnp.einsum("...lsmt,lmtk->...lsmk", parts, books, preferred_element_type=F32)
    wide = parts.astype(F32)
    own = jnp.sum(wide * wide, axis=-1)
    word = jnp.sum(jnp.square(books.astype(F32)), axis=2)
    return (own[..., None] - 2.0 * cross + word[:, None, :, :]) / width


def any_narrow(queries, probes, cell_slot, centroids, rotations, codebooks):
    q_dev, probe_count = probes.shape
    cells_all = cell_slot.shape[0]
    cell_dev = centroids.shape[0]
    depth = queries.shape[1]
    most = most_of(q_dev, probe_count, cells_all)
    owners = lax.axis_size("cells")
    span = jnp.arange(cells_all, dtype=jnp.int32)
    owner_hot = (cell_slot[:, None] == span[None, :]).astype(jnp.int32)
    probe_hot = (probes.reshape(-1)[:, None] == span[None, :]).astype(jnp.int32)
    position_hot = jnp.dot(probe_hot, owner_hot)
    rank = jnp.sum((jnp.cumsum(position_hot, axis=0) - position_hot) * position_hot, axis=1)
    position = jnp.dot(position_hot, span)
    slot = position * most + rank
    slot_span = jnp.arange(cells_all * most, dtype=jnp.int32)
    assign = jnp.sum(
        (slot[:, None] == slot_span[None, :])
        .astype(jnp.int32)
        .reshape(q_dev, probe_count, cells_all * most),
        axis=1,
    )
    send = jnp.einsum(
        "qs,qd->sd", assign.astype(BF16), queries, preferred_element_type=F32
    ).astype(BF16)
    valid = jnp.sum(assign, axis=0).astype(BF16)
    rows = lax.all_to_all(
        send.reshape(owners, cell_dev * most, depth), "cells", split_axis=0, concat_axis=0, tiled=True
    ).reshape(owners, cell_dev, most, depth)
    marks = lax.all_to_all(
        valid.reshape(owners, cell_dev * most), "cells", split_axis=0, concat_axis=0, tiled=True
    ).reshape(owners, cell_dev, most)
    residual = (rows.astype(F32) - centroids[None, :, None, :]).astype(BF16)
    rotated = jnp.einsum(
        "nilsd,lde->nilse",
        lax.all_gather(residual[None], "narrow", axis=0, tiled=True),
        rotations,
        preferred_element_type=F32,
    ).astype(BF16)
    gathered = subspace_tables(rotated, codebooks).astype(BF16)
    mine = lax.all_to_all(gathered, "narrow", split_axis=0, concat_axis=4, tiled=True)[0]
    table = mine * marks[..., None, None]
    return table.reshape((1, 1, owners * cell_dev * most) + table.shape[-2:])


def solution(mesh):
    return jax.shard_map(
        two_narrow if mesh.shape["narrow"] == mesh.shape["groups"] == 2 and mesh.shape["cells"] % 2 == 0 else any_narrow,
        mesh=mesh,
        in_specs=(
            P(("groups", "cells", "narrow"), None),
            P(("groups", "cells", "narrow"), None),
            P(),
            P("cells", None),
            P("cells", None, "narrow"),
            P("cells", "narrow", None, None),
        ),
        out_specs=P(("groups", "cells"), "narrow", None, None, None),
        check_vma=False,
    )
```

```python
import functools

import jax
import jax.numpy as jnp
from jax import lax
from jax.experimental import pallas as pl
from jax.experimental.pallas import tpu as pltpu
from jax.sharding import PartitionSpec as P

MESH = pl.DeviceIdType.MESH
F32 = jnp.float32
BF16 = jnp.bfloat16
LANES = 128
TABLE_STEPS = 1


def most_of(q_dev, probe_count, cells_all):
    return min(q_dev, max(2, 2 * q_dev * probe_count // cells_all))


def exchange_kernel(
    owners, most, slot_hbm, queries_hbm, probes_hbm, centroids_hbm, rotations, books,
    x_out, books_out, marks_out,
    blocks, turn, x_send, slot_of, probes, centroids,
    q_send_sem, q_recv_sem, b_send_sem, b_recv_sem, y_send_sem, y_recv_sem, x_send_sem, x_recv_sem, local_sem,
):
    q_dev, depth = queries_hbm.shape
    probe_count = probes.shape[1]
    cell_dev, half_m = books.shape[:2]
    half = rotations.shape[2]
    cells_all = slot_of.shape[0]
    rows = owners * q_dev
    slots = owners * most
    pieces = b_send_sem.shape[0]
    step = half_m // pieces
    g = lax.axis_index("groups")
    j = lax.axis_index("cells")
    n = lax.axis_index("narrow")
    other = 1 - n

    hops = range(1, owners // 2)
    beside = j + 1 - 2 * lax.rem(j, 2)
    facing = (g, j, other)
    paired = (g, beside, n)

    def ahead(d):
        return (g, lax.rem(j + 2 * d, owners), n)

    def behind(cell, d):
        return lax.rem(cell + owners - 2 * d, owners)

    across = (1 - g, j, n)
    barrier = pltpu.get_barrier_semaphore()
    partners = [facing, paired, across] + [ahead(d) for d in hops]
    for partner in partners:
        pl.semaphore_signal(barrier, inc=1, device_id=partner, device_id_type=MESH)

    loads = [
        pltpu.make_async_copy(src, dst, local_sem.at[i])
        for i, (src, dst) in enumerate(
            [
                (queries_hbm, blocks.at[n, j, :, pl.ds(0, depth)]),
                (probes_hbm, probes),
                (slot_hbm, slot_of),
                (centroids_hbm, centroids),
                (rotations, turn),
            ]
        )
    ]
    for load in loads:
        load.start()
    loads[1].wait()
    tail = jnp.concatenate(
        [probes[...].astype(F32), jnp.zeros((q_dev, LANES - probe_count), F32)], axis=1
    )
    blocks[n, j, :, depth:] = tail.astype(BF16)
    loads[0].wait()
    pl.semaphore_wait(barrier, len(partners))

    def block_copy(k, column_at, cell, device):
        return pltpu.make_async_remote_copy(
            src_ref=blocks.at[column_at, cell],
            dst_ref=blocks.at[column_at, cell],
            send_sem=q_send_sem.at[k],
            recv_sem=q_recv_sem.at[k],
            device_id=device,
            device_id_type=MESH,
        )

    sends = []

    def send(k, column_at, cell, device):
        copy = block_copy(k, column_at, cell, device)
        copy.start()
        sends.append(copy)

    count = 2 * len(hops) + 1

    def from_behind(c, d):
        return 1 + c * count + d - 1

    def from_paired(c, d):
        return 1 + c * count + len(hops) + d

    columns = (n, other)
    send(0, n, j, facing)
    for d in hops:
        send(from_behind(0, d), n, j, ahead(d))
    send(from_paired(0, 0), n, j, paired)
    firsts = []
    for p in range(pieces):
        copy = pltpu.make_async_remote_copy(
            src_ref=books.at[g, pl.ds(p * step, step)],
            dst_ref=books_out.at[g, pl.ds(p * step, step)],
            send_sem=b_send_sem.at[p],
            recv_sem=b_recv_sem.at[p],
            device_id=(g, j, other),
            device_id_type=MESH,
        )
        copy.start()
        firsts.append(copy)
    relays = []

    def relay(p):
        firsts[p].wait_recv()
        piece = books_out.at[g, pl.ds(p * step, step)]
        copy = pltpu.make_async_remote_copy(
            src_ref=piece,
            dst_ref=piece,
            send_sem=y_send_sem.at[p],
            recv_sem=y_recv_sem.at[p],
            device_id=across,
            device_id_type=MESH,
        )
        copy.start()
        relays.append(copy)

    block_copy(0, other, j, facing).wait_recv()
    for d in hops:
        send(from_behind(1, d), other, j, ahead(d))
    send(from_paired(1, 0), other, j, paired)

    def pass_on(c):
        for d in hops:
            block_copy(from_behind(c, d), columns[c], behind(j, d), paired).wait_recv()
            send(from_paired(c, d), columns[c], behind(j, d), paired)

    def arrived(c):
        for d in range(owners // 2):
            block_copy(
                from_paired(c, d), columns[c], behind(beside, d), paired
            ).wait_recv()

    row = lax.broadcasted_iota(jnp.int32, (rows, rows), 0)
    col = lax.broadcasted_iota(jnp.int32, (rows, rows), 1)
    earlier = ((row < col) & (row // q_dev == col // q_dev)).astype(F32).astype(BF16)
    slot_row = lax.broadcasted_iota(jnp.int32, (slots, rows), 0)
    slot_col = lax.broadcasted_iota(jnp.int32, (slots, rows), 1)
    same = (slot_row // most == slot_col // q_dev).astype(F32)
    place = (slot_row % most).astype(F32)

    def cell_at(position):
        cell = jnp.int32(0)
        for c in range(cells_all):
            cell = cell + jnp.where(slot_of[c] == position, c, 0)
        return cell

    loads[2].wait()
    loads[3].wait()
    cells = [cell_at(j * cell_dev + l).astype(F32) for l in range(cell_dev)]

    def column(which):
        wide = blocks[which].astype(F32).reshape(rows, depth + LANES)
        named = wide[:, depth:]
        lane = lax.broadcasted_iota(jnp.int32, (rows, LANES), 1) < probe_count
        for l in range(cell_dev):
            hit = ((named == cells[l]) & lane).astype(F32).astype(BF16)
            hits = lax.dot_general(
                jnp.ones((8, LANES), BF16), hit, (((1,), (1,)), ((), ())),
                preferred_element_type=F32,
            )
            rank = jnp.dot(hits.astype(BF16), earlier, preferred_element_type=F32)
            pick = (place == rank[:1]).astype(F32) * hits[:1] * same
            residual = (wide[:, :depth] - centroids[l : l + 1]).astype(BF16)
            rotated = jnp.dot(residual, turn[l], preferred_element_type=F32).astype(BF16)
            x = jnp.dot(pick.astype(BF16), rotated, preferred_element_type=F32).astype(BF16)
            yield x, pick

    here = pl.ds(pl.multiple_of(n * half, LANES), half)
    relay(0)
    pass_on(1)
    relay(1)
    pass_on(0)
    for p in range(2, pieces - 1):
        relay(p)
    loads[4].wait()
    arrived(1)
    relay(pieces - 1)
    x_copies = []
    for l, (x, _) in enumerate(column(other)):
        x_send[l] = x
        copy = pltpu.make_async_remote_copy(
            src_ref=x_send.at[l],
            dst_ref=x_out.at[l, :, here],
            send_sem=x_send_sem.at[l],
            recv_sem=x_recv_sem.at[l],
            device_id=facing,
            device_id_type=MESH,
        )
        copy.start()
        x_copies.append(copy)
    arrived(0)
    for l, (x, pick) in enumerate(column(n)):
        x_out[l, :, here] = x
        marks_out[l] = jnp.broadcast_to(
            jnp.sum(pick, axis=1, keepdims=True), marks_out.shape[1:]
        )
    for copy in sends + firsts:
        copy.wait_send()
    for copy in x_copies + relays:
        copy.wait()


def table_kernel(x_ref, own_ref, far_ref, marks_ref, out_ref):
    _, half_m, width, words = own_ref.shape
    slots = x_ref.shape[1]
    blocks, _, most = out_ref.shape[:3]
    group = 16
    span = group * width
    scale = 1.0 / width
    n = lax.axis_index("narrow")

    lane = lax.broadcasted_iota(jnp.int32, (group, span), 1)
    row = lax.broadcasted_iota(jnp.int32, (group, span), 0)
    mask = (lane // width == row).astype(F32)
    marks = jnp.concatenate([marks_ref[0]] * (words // LANES), axis=1)

    for books_ref, which in ((own_ref, n), (far_ref, 1 - n)):
        for piece in range(half_m // group):
            start = which * half_m + piece * group
            books = books_ref[0, piece * group : (piece + 1) * group]
            wide = books.astype(F32)
            word = jnp.sum(wide * wide, axis=1) * scale
            x = x_ref[0, :, pl.ds(pl.multiple_of(start * width, span), span)].astype(F32)
            spread = x[:, None, :] * mask[None]
            own = jnp.sum(spread * spread, axis=2, keepdims=True) * scale
            table = jnp.dot(
                (spread * (-2.0 * scale)).astype(BF16).reshape(slots * group, span),
                books.reshape(span, words),
                preferred_element_type=F32,
            ).reshape(slots, group, words)
            table = table + (own + word[None] * marks[:, None, :])
            out_ref[:, :, :, pl.ds(pl.multiple_of(start, group), group), :] = table.astype(
                BF16
            ).reshape(blocks, 1, most, group, words)


def two_narrow(queries, probes, cell_slot, centroids, rotations, codebooks):
    q_dev, probe_count = probes.shape
    cells_all = cell_slot.shape[0]
    cell_dev, half_m, width, words = codebooks.shape
    depth = queries.shape[1]
    half = rotations.shape[2]
    owners = lax.axis_size("cells")
    most = most_of(q_dev, probe_count, cells_all)
    slots = owners * most
    peers = 2 * owners - 1
    vmem = pl.BlockSpec(memory_space=pltpu.VMEM)
    pieces = 4
    x, books, marks = pl.pallas_call(
        functools.partial(exchange_kernel, owners, most),
        name="exchange",
        out_shape=(
            jax.ShapeDtypeStruct((cell_dev, slots, depth), BF16),
            jax.ShapeDtypeStruct(codebooks.shape, BF16),
            jax.ShapeDtypeStruct((cell_dev, slots, LANES), F32),
        ),
        in_specs=[pl.BlockSpec(memory_space=pltpu.HBM)] * 6,
        out_specs=(vmem, pl.BlockSpec(memory_space=pl.ANY), vmem),
        scratch_shapes=[
            pltpu.VMEM((2, owners, q_dev, depth + LANES), BF16),
            pltpu.VMEM(rotations.shape, BF16),
            pltpu.VMEM((cell_dev, slots, half), BF16),
            pltpu.SMEM(cell_slot.shape, jnp.int32),
            pltpu.VMEM(probes.shape, jnp.int32),
            pltpu.VMEM(centroids.shape, F32),
            pltpu.SemaphoreType.DMA((peers,)),
            pltpu.SemaphoreType.DMA((peers,)),
            pltpu.SemaphoreType.DMA((pieces,)),
            pltpu.SemaphoreType.DMA((pieces,)),
            pltpu.SemaphoreType.DMA((pieces,)),
            pltpu.SemaphoreType.DMA((pieces,)),
            pltpu.SemaphoreType.DMA((cell_dev,)),
            pltpu.SemaphoreType.DMA((cell_dev,)),
            pltpu.SemaphoreType.DMA((5,)),
        ],
        compiler_params=pltpu.CompilerParams(
            collective_id=0, has_side_effects=True, vmem_limit_bytes=64 << 20
        ),
    )(cell_slot, queries, probes, centroids, rotations, codebooks)

    part = max(owners // TABLE_STEPS, 1)
    table = pl.pallas_call(
        table_kernel,
        name="tables",
        grid=(cell_dev, owners // part),
        out_shape=jax.ShapeDtypeStruct((owners, cell_dev, most, 2 * half_m, words), BF16),
        in_specs=[
            pl.BlockSpec((1, part * most, depth), lambda l, i: (l, i, 0)),
            pl.BlockSpec((1, half_m, width, words), lambda l, i: (l, 0, 0, 0)),
            pl.BlockSpec((1, half_m, width, words), lambda l, i: (l, 0, 0, 0)),
            pl.BlockSpec((1, part * most, LANES), lambda l, i: (l, i, 0)),
        ],
        out_specs=pl.BlockSpec(
            (part, 1, most, 2 * half_m, words), lambda l, i: (i, l, 0, 0, 0)
        ),
        compiler_params=pltpu.CompilerParams(vmem_limit_bytes=64 << 20),
    )(x, codebooks, books, marks)
    return table.reshape(1, 1, owners * cell_dev * most, 2 * half_m, words)


def subspace_tables(rotated, books):
    width = books.shape[2]
    parts = rotated.reshape(rotated.shape[:-1] + (books.shape[1], width))
    cross = jnp.einsum("...lsmt,lmtk->...lsmk", parts, books, preferred_element_type=F32)
    wide = parts.astype(F32)
    own = jnp.sum(wide * wide, axis=-1)
    word = jnp.sum(jnp.square(books.astype(F32)), axis=2)
    return (own[..., None] - 2.0 * cross + word[:, None, :, :]) / width


def any_narrow(queries, probes, cell_slot, centroids, rotations, codebooks):
    q_dev, probe_count = probes.shape
    cells_all = cell_slot.shape[0]
    cell_dev = centroids.shape[0]
    depth = queries.shape[1]
    most = most_of(q_dev, probe_count, cells_all)
    owners = lax.axis_size("cells")
    span = jnp.arange(cells_all, dtype=jnp.int32)
    owner_hot = (cell_slot[:, None] == span[None, :]).astype(jnp.int32)
    probe_hot = (probes.reshape(-1)[:, None] == span[None, :]).astype(jnp.int32)
    position_hot = jnp.dot(probe_hot, owner_hot)
    rank = jnp.sum((jnp.cumsum(position_hot, axis=0) - position_hot) * position_hot, axis=1)
    position = jnp.dot(position_hot, span)
    slot = position * most + rank
    slot_span = jnp.arange(cells_all * most, dtype=jnp.int32)
    assign = jnp.sum(
        (slot[:, None] == slot_span[None, :])
        .astype(jnp.int32)
        .reshape(q_dev, probe_count, cells_all * most),
        axis=1,
    )
    send = jnp.einsum(
        "qs,qd->sd", assign.astype(BF16), queries, preferred_element_type=F32
    ).astype(BF16)
    valid = jnp.sum(assign, axis=0).astype(BF16)
    rows = lax.all_to_all(
        send.reshape(owners, cell_dev * most, depth), "cells", split_axis=0, concat_axis=0, tiled=True
    ).reshape(owners, cell_dev, most, depth)
    marks = lax.all_to_all(
        valid.reshape(owners, cell_dev * most), "cells", split_axis=0, concat_axis=0, tiled=True
    ).reshape(owners, cell_dev, most)
    residual = (rows.astype(F32) - centroids[None, :, None, :]).astype(BF16)
    rotated = jnp.einsum(
        "nilsd,lde->nilse",
        lax.all_gather(residual[None], "narrow", axis=0, tiled=True),
        rotations,
        preferred_element_type=F32,
    ).astype(BF16)
    gathered = subspace_tables(rotated, codebooks).astype(BF16)
    mine = lax.all_to_all(gathered, "narrow", split_axis=0, concat_axis=4, tiled=True)[0]
    table = mine * marks[..., None, None]
    return table.reshape((1, 1, owners * cell_dev * most) + table.shape[-2:])


def solution(mesh):
    return jax.shard_map(
        two_narrow if mesh.shape["narrow"] == mesh.shape["groups"] == 2 and mesh.shape["cells"] % 2 == 0 else any_narrow,
        mesh=mesh,
        in_specs=(
            P(("groups", "cells", "narrow"), None),
            P(("groups", "cells", "narrow"), None),
            P(),
            P("cells", None),
            P("cells", None, "narrow"),
            P("cells", "narrow", None, None),
        ),
        out_specs=P(("groups", "cells"), "narrow", None, None, None),
        check_vma=False,
    )
```
